128 devices in a mesh: comp: 2 (over z_hi), tile: 64 (over y, z_lo, x, core).
Axes of the slice: x: 4, y: 4, z: 4 (z_hi: 2, z_lo: 2; z = z_hi * 2 + z_lo), core: 2. Of those that a mesh axis runs over, the one named last changes fastest.
Arguments:
- fields: float32 [2, 14, 64, 32768], P('comp', None, None, 'tile'), may hold values from -5 to 5
- velocity: float32 [2, 2, 14, 64, 32768], P('comp', None, None, None, 'tile'), may hold values from -3 to 3
- mixing: float32 [2, 13, 64, 32768], P('comp', None, None, 'tile'), may hold values from 0.1 to 3
- surface_mask: int32 [2, 64, 32768], P('comp', None, 'tile'), may hold values 0 or 1
- intersection_ids: int32 [2, 16384, 2], P('comp', 'tile'), may hold values from 0 to 16383, as said below
- intersection_weights: bfloat16 [2, 16384, 2, 128, 128], P('comp', 'tile'), may hold values from -0.375 to 0.375
Outputs:
- advanced: float32 [2, 14, 64, 32768], P('comp', None, None, 'tile')
- coupled: float32 [2, 2, 64, 32768], P('comp', None, None, 'tile')
The draws below stay inside these ranges and needn't reach their ends.
Inputs may be any that keep to these rules, and one draw needn't show every extreme that they name: `intersection_ids`: the 2 sources of a destination block on tile t are blocks of the tiles t - 1, t and t + 1 (the last and the first tile lie beside each other); a source may repeat.
All inputs are finite; a program needn't handle non-finite values. No bound on the sum of `surface_mask` on one device may be relied on, other than what follows from the above.
Results may differ from the reference program's by a relative error of at most 0.0029.
Values may be sent and summed in bfloat16 or wider, within the bound.
A program may use at most 128 MiB of HBM per device.

```python
import math
import jax
import jax.numpy as jnp
import numpy as np
from jax import lax

LEV = 14
BLOCK = 128
PAIRS = 2
FIELDS = 2
ROWS = 64
COLS = 512
ALLCOLS = 32768
BLOCKS = 256
ALLBLOCKS = 16384
N_TILE = 64


def draw_intersection_ids(key, part):
    key = jax.random.fold_in(key, 11)
    key_offsets, key_blocks = jax.random.split(key)
    offsets = jax.random.randint(key_offsets, (2, ALLBLOCKS, PAIRS), -1, 2)
    local_block = jax.random.randint(key_blocks, (2, ALLBLOCKS, PAIRS), 0, BLOCKS)
    home_tile = (jnp.arange(ALLBLOCKS) // BLOCKS)[None, :, None]
    tile_total = ALLBLOCKS // BLOCKS
    source_ids = (home_tile + offsets) % tile_total * BLOCKS + local_block
    source_ids = source_ids.at[:, 0, 0].set(0)
    source_ids = source_ids.at[:, ALLBLOCKS - 1, 0].set(ALLBLOCKS - 1)
    return source_ids.astype(jnp.int32)


def plant(values, key, least, largest):
    spot = [jax.random.randint(jax.random.fold_in(key, axis), (), 0, length) for axis, length in enumerate(values.shape)]
    widest = values.shape.index(max(values.shape))
    next_to = spot[:widest] + [(spot[widest] + 1) % values.shape[widest]] + spot[widest + 1:]
    return values.at[tuple(spot)].set(least).at[tuple(next_to)].set(largest)


def steps_of(own_key, dims, cuts, smallest, high):
    gain, own = 1.0, jax.random.fold_in(own_key, 6)
    for dim, parts in cuts:
        heights = jnp.exp(jax.random.uniform(jax.random.fold_in(own, dim), (parts,), jnp.float32, smallest / len(cuts), high / len(cuts)))
        gain = gain * jnp.repeat(heights, dims[dim] // parts).reshape([-1 if axis == dim else 1 for axis in range(len(dims))])
    return gain


def noise(own_key, shape, deviation, most, cuts=(), dtype=jnp.bfloat16):
    values = deviation * jax.random.normal(own_key, shape, jnp.float32)
    if cuts:
        values = values * steps_of(own_key, shape, cuts, -0.22, 0.18)
    return jnp.clip(values, -most, most).astype(dtype)


def setup_inputs(seed: int = 0) -> dict:
    key_of = jax.random.split(jax.random.key(seed), 7)
    return {
        "fields": noise(key_of[0], (2, LEV, ROWS, ALLCOLS), 1.0, 5.0, ((0, 2), (3, 64)), jnp.float32),
        "velocity": noise(key_of[1], (2, 2, LEV, ROWS, ALLCOLS), 0.8, 3.0, ((0, 2), (4, 64)), jnp.float32),
        "mixing": jnp.clip(jnp.exp(math.log(3.0) - 3.4011974 * jax.random.uniform(key_of[2], (2, LEV - 1, ROWS, ALLCOLS), jnp.float32) ** steps_of(key_of[2], (2, LEV - 1, ROWS, ALLCOLS), ((0, 2), (3, 64)), -0.2, 0.2)), 0.1, 3.0),
        "surface_mask": plant((jax.random.randint(key_of[3], (2, ROWS, ALLCOLS), 0, 10) < 7).astype(jnp.int32), jax.random.fold_in(key_of[3], 1), 0, 1),
        "intersection_ids": draw_intersection_ids(jax.random.fold_in(key_of[6], 71), 0),
        "intersection_weights": noise(key_of[5], (2, ALLBLOCKS, PAIRS, BLOCK, BLOCK), (PAIRS * BLOCK) ** -0.5, 0.375, ((0, 2), (1, 64))),
    }


atmos_advect = 0.08
ocean_advect = 0.25
ocean_diffuse = 0.15
heat_exchange = 0.5
highest = lax.Precision.HIGHEST

def gll_table():
    node_list = [-1.0, -1.0 / math.sqrt(5.0), 1.0 / math.sqrt(5.0), 1.0]
    bary_weights = []
    for first_node in range(4):
        product_value = 1.0
        for other_node in range(4):
            if other_node != first_node:
                product_value = product_value * (node_list[first_node] - node_list[other_node])
        bary_weights.append(product_value)
    deriv_rows = []
    for first_node in range(4):
        entries = []
        for second_node in range(4):
            if first_node == second_node:
                entry_value = 0.0
                for other_node in range(4):
                    if other_node != first_node:
                        entry_value = entry_value + 1.0 / (node_list[first_node] - node_list[other_node])
            else:
                entry_value = bary_weights[first_node] / bary_weights[second_node] / (node_list[first_node] - node_list[second_node])
            entries.append(entry_value)
        deriv_rows.append(entries)
    return np.array(deriv_rows)

def vertical_mix(values, coeffs):
    level_count = values.shape[0]
    zero_slab = jnp.zeros_like(values[0])
    factors = []
    partial_sol = []
    for level_index in range(level_count):
        coeff_above = coeffs[level_index - 1] if level_index > 0 else zero_slab
        coeff_below = coeffs[level_index] if level_index < level_count - 1 else zero_slab
        diagonal = 1.0 + coeff_above + coeff_below
        if level_index == 0:
            denom_value = diagonal
            carried = values[0] / denom_value
        else:
            denom_value = diagonal + coeff_above * factors[level_index - 1]
            carried = (values[level_index] + coeff_above * partial_sol[level_index - 1]) / denom_value
        factors.append(-coeff_below / denom_value)
        partial_sol.append(carried)
    result_levels = [partial_sol[level_count - 1]]
    for level_index in range(level_count - 2, -1, -1):
        result_levels.append(partial_sol[level_index] - factors[level_index] * result_levels[-1])
    return jnp.stack(result_levels[::-1])

def columns_mean(values, east_side, west_side):
    col_phase = jnp.arange(values.shape[2]) % 4
    return jnp.where(col_phase == 3, 0.5 * (values + east_side), jnp.where(col_phase == 0, 0.5 * (values + west_side), values))

def rows_and_fold(col_mean, mirror_top):
    row_count = col_mean.shape[1]
    row_ids = jnp.arange(row_count)[:, None]
    row_phase = row_ids % 4
    upper_rows = jnp.concatenate([col_mean[:, 1:], col_mean[:, -1:]], axis=1)
    lower_rows = jnp.concatenate([col_mean[:, :1], col_mean[:, :-1]], axis=1)
    averaged = jnp.where((row_phase == 3) & (row_ids < row_count - 1), 0.5 * (col_mean + upper_rows), jnp.where((row_phase == 0) & (row_ids > 0), 0.5 * (col_mean + lower_rows), col_mean))
    return averaged.at[:, row_count - 1].set(0.5 * (col_mean[:, row_count - 1] + mirror_top))

def ocean_tendency(values, currents, wet_here, east_side, west_side, north_side, south_side, east_wet, west_wet, north_wet, south_wet):
    east_diff = east_wet * (east_side - values)
    west_diff = west_wet * (west_side - values)
    north_diff = north_wet * (north_side - values)
    south_diff = south_wet * (south_side - values)
    return wet_here * (ocean_diffuse * (east_diff + west_diff + north_diff + south_diff) - ocean_advect * (currents[0] * (east_diff - west_diff) + currents[1] * (north_diff - south_diff)))

def atmos_tendency(values, wind_field, bottom_rate, target, deriv_small):
    along = jnp.einsum('lrem,im->lrei', values.reshape(LEV, ROWS, ALLCOLS // 4, 4), deriv_small, precision=highest).reshape(values.shape)
    across = jnp.einsum('lemc,jm->lejc', values.reshape(LEV, ROWS // 4, 4, ALLCOLS), deriv_small, precision=highest).reshape(values.shape)
    tendency = -atmos_advect * (wind_field[0] * along + wind_field[1] * across)
    return tendency.at[LEV - 1].add(bottom_rate * (target - values[LEV - 1]))

def to_blocks(surface):
    split = surface.reshape(FIELDS, ROWS, N_TILE, COLS).transpose(0, 2, 1, 3)
    return split.reshape(FIELDS, ALLBLOCKS, BLOCK)

def from_blocks(blocks):
    split = blocks.reshape(FIELDS, N_TILE, ROWS, COLS).transpose(0, 2, 1, 3)
    return split.reshape(FIELDS, ROWS, ALLCOLS)

def regrid(weight_tiles, id_lists, source):
    weight_parts = weight_tiles.reshape(N_TILE, BLOCKS, PAIRS, BLOCK, BLOCK)
    id_parts = id_lists.reshape(N_TILE, BLOCKS, PAIRS)

    def one_tile(operands):
        weight_part, id_part = operands
        picked = jnp.take(source, id_part.reshape(-1).astype(jnp.int32), axis=1)
        picked = picked.reshape(FIELDS, BLOCKS, PAIRS, BLOCK)
        return jnp.einsum('bkpq,fbkq->fbp', weight_part.astype(jnp.float32), picked.astype(jnp.float32), precision=highest)
    result = lax.map(one_tile, (weight_parts, id_parts))
    return result.transpose(1, 0, 2, 3).reshape(FIELDS, ALLBLOCKS, BLOCK)

def reference(fields, velocity, mixing, surface_mask, intersection_ids, intersection_weights):
    wet_all = surface_mask.astype(jnp.float32)
    deriv_small = jnp.asarray(gll_table(), jnp.float32)
    surf_atmos = jnp.stack([fields[0, LEV - 1], velocity[0, 0, LEV - 1]])
    surf_ocean = jnp.stack([fields[1, 0], velocity[1, 0, 0]])
    blocks_atmos = to_blocks(surf_atmos).astype(jnp.bfloat16)
    blocks_ocean = to_blocks(surf_ocean).astype(jnp.bfloat16)
    coupled_atmos = from_blocks(regrid(intersection_weights[0], intersection_ids[0], blocks_ocean))
    coupled_ocean = from_blocks(regrid(intersection_weights[1], intersection_ids[1], blocks_atmos))
    bottom_rate = heat_exchange * (1.0 + jnp.abs(velocity[0, 0, LEV - 1] - coupled_atmos[1])) * wet_all[0]
    atmos = fields[0]
    for round_index in range(2):
        stepped = atmos + atmos_tendency(atmos, velocity[0], bottom_rate, coupled_atmos[0], deriv_small)
        col_mean = columns_mean(stepped, jnp.roll(stepped, -1, axis=2), jnp.roll(stepped, 1, axis=2))
        assembled = rows_and_fold(col_mean, col_mean[:, ROWS - 1, ::-1])
        atmos = vertical_mix(assembled, mixing[0])
    wet_ocean = wet_all[1]
    currents = velocity[1]

    def ocean_eval(values):
        north_side = jnp.concatenate([values[:, 1:], values[:, -1:, ::-1]], axis=1)
        north_wet = jnp.concatenate([wet_ocean[1:], wet_ocean[-1:, ::-1]], axis=0)
        south_side = jnp.concatenate([values[:, :1], values[:, :-1]], axis=1)
        south_wet = jnp.concatenate([jnp.zeros_like(wet_ocean[:1]), wet_ocean[:-1]], axis=0)
        return ocean_tendency(values, currents, wet_ocean, jnp.roll(values, -1, axis=2), jnp.roll(values, 1, axis=2), north_side, south_side, jnp.roll(wet_ocean, -1, axis=1), jnp.roll(wet_ocean, 1, axis=1), north_wet, south_wet)
    ocean_start = fields[1]
    forcing = heat_exchange * (1.0 + jnp.abs(coupled_ocean[1] - velocity[1, 0, 0])) * (coupled_ocean[0] - ocean_start[0]) * wet_ocean
    first_tend = ocean_eval(ocean_start)
    middle = (ocean_start + first_tend).at[0].add(forcing)
    second_tend = ocean_eval(middle)
    ocean = vertical_mix((ocean_start + 0.5 * (first_tend + second_tend)).at[0].add(forcing), mixing[1])
    return (jnp.stack([atmos, ocean]), jnp.stack([coupled_atmos, coupled_ocean]))
```

```python
import functools
import math

import jax
import jax.numpy as jnp
import numpy as np
from jax import lax
from jax.experimental import pallas as pl
from jax.experimental.pallas import tpu as pltpu
from jax.sharding import PartitionSpec as P

LEV = 14
TILES = 8
SUB = 8
COLS = 512
LANES = 128
GROUPS = 4
BLOCKS = 256
N_TILE = 64
MESH = pl.DeviceIdType.MESH
F32 = jnp.float32
BF16 = jnp.bfloat16


def gll_table():
    nodes = [-1.0, -1.0 / math.sqrt(5.0), 1.0 / math.sqrt(5.0), 1.0]
    weights = [math.prod(nodes[i] - nodes[j] for j in range(4) if j != i) for i in range(4)]
    table = np.zeros((4, 4))
    for i in range(4):
        for j in range(4):
            if i == j:
                table[i, j] = sum(1.0 / (nodes[i] - nodes[k]) for k in range(4) if k != i)
            else:
                table[i, j] = weights[i] / weights[j] / (nodes[i] - nodes[j])
    return table


def along_matrix():
    full = np.kron(np.eye(LANES // 4), gll_table().T).astype(np.float32)
    high = full.astype(jnp.bfloat16)
    low = (full - high.astype(np.float32)).astype(jnp.bfloat16)
    top = np.concatenate([high, low], axis=1)
    bottom = np.concatenate([high, np.zeros_like(low)], axis=1)
    return np.concatenate([top, bottom], axis=0)


def across_table():
    table = gll_table()
    coefs = np.zeros((7, SUB, LANES), np.float32)
    for row in range(SUB):
        for offset in range(-3, 4):
            if 0 <= row % 4 + offset < 4:
                coefs[offset + 3, row, :] = table[row % 4, row % 4 + offset]
    return coefs


def kernel(
    ids, coef, dmat, fields, velocity, mixing, mask_in, weights,
    adv_out, cpl_out,
    u, vel, kap, msk, wbuf, surf, src, winb, win, cpl, st, first, inv,
    pos, pack_w, pack_e, top, halo_w, halo_e, mirror, corner_w, corner_e,
    lsem, wsem, osem, e0s, e0r, xs, xr,
):
    comp = lax.axis_index("comp")
    tile = lax.axis_index("tile")
    other = 1 - comp
    east = lax.rem(tile + 1, N_TILE)
    west = lax.rem(tile + N_TILE - 1, N_TILE)
    fold = N_TILE - 1 - tile
    fold_lo = lax.rem(fold + N_TILE - 1, N_TILE)
    fold_hi = lax.rem(fold + 1, N_TILE)
    is_atmos = comp == 0
    level_s = jnp.where(is_atmos, LEV - 1, 0)

    def local(src_ref, dst_ref, sem):
        return pltpu.make_async_copy(src_ref, dst_ref, sem)

    def remote(src_ref, dst_ref, send, recv, target):
        return pltpu.make_async_remote_copy(
            src_ref=src_ref, dst_ref=dst_ref, send_sem=send, recv_sem=recv,
            device_id=target, device_id_type=MESH,
        )

    loads = [
        local(fields.at[level_s], surf.at[0], lsem.at[0]),
        local(velocity.at[0, level_s], surf.at[1], lsem.at[1]),
        local(fields, u, lsem.at[2]),
        local(mask_in, msk, lsem.at[3]),
        local(mixing, kap, lsem.at[4]),
        local(velocity, vel, lsem.at[5]),
    ]
    order = (0, 3, 1, 2)
    wloads = [local(weights.at[:, :, j], wbuf.at[j], wsem.at[j]) for j in range(GROUPS)]
    for load in loads:
        load.start()
    for j in order:
        wloads[j].start()

    barrier = pltpu.get_barrier_semaphore()
    for target in (
        (other, tile), (other, east), (other, west), (comp, east), (comp, west), (comp, fold),
    ):
        pl.semaphore_signal(barrier, inc=1, device_id=target, device_id_type=MESH)

    @pl.when(fold_lo != tile)
    def _():
        pl.semaphore_signal(barrier, inc=1, device_id=(comp, fold_lo), device_id_type=MESH)

    @pl.when(fold_hi != tile)
    def _():
        pl.semaphore_signal(barrier, inc=1, device_id=(comp, fold_hi), device_id_type=MESH)

    loads[0].wait()
    loads[1].wait()
    for f in range(2):
        for j in range(GROUPS):
            src[f, j] = surf[f, :, :, j * LANES:(j + 1) * LANES].reshape(64, LANES).astype(BF16)

    selfs = jnp.where(fold_lo == tile, 1, 0) + jnp.where(fold_hi == tile, 1, 0)
    pl.semaphore_wait(barrier, 8 - selfs)

    sends = [
        remote(src, winb.at[1], e0s.at[1], e0r.at[1], (other, tile)),
        remote(src, winb.at[0], e0s.at[0], e0r.at[0], (other, east)),
        remote(src, winb.at[2], e0s.at[2], e0r.at[2], (other, west)),
    ]
    for send in sends:
        send.start()

    lane = lax.broadcasted_iota(jnp.int32, (SUB, LANES), 1)
    lane_w = lax.broadcasted_iota(jnp.int32, (SUB, COLS), 1)
    row_w = lax.broadcasted_iota(jnp.int32, (SUB, COLS), 0)
    phase_col = lane_w & 3
    phase_row = row_w & 3
    flip = (LANES - 1) - lane

    def positions(n, carry):
        for s in range(8):
            ident = ids[n * 8 + s]
            relative = (lax.shift_right_logical(ident, 8) - tile + 1 + N_TILE) & (N_TILE - 1)
            relative = jnp.minimum(relative, 2)
            block = ident & (BLOCKS - 1)
            pos[n * 8 + s] = relative * BLOCKS + (block & 3) * 64 + lax.shift_right_logical(block, 2)
        return carry

    def factors(i, carry):
        above = None
        ratio = None
        for l in range(LEV):
            diagonal = 1.0
            if l < LEV - 1:
                below = kap[l, i]
                diagonal = below + 1.0
            if l > 0:
                diagonal = diagonal + above * (1.0 - ratio)
            inverse = 1.0 / diagonal
            inv[l, i] = inverse
            if l < LEV - 1:
                ratio = below * inverse
                above = below
        return carry

    def tendency(i, carry):
        for j in range(GROUPS):
            span = slice(j * LANES, (j + 1) * LANES)
            x = u[:, i, :, span]
            flat = x.reshape(LEV * SUB, LANES)
            high = flat.astype(BF16)
            low = (flat - high.astype(F32)).astype(BF16)
            product = jnp.dot(
                jnp.concatenate([high, low], axis=1), dmat[...], preferred_element_type=F32
            )
            along = (product[:, :LANES] + product[:, LANES:]).reshape(LEV, SUB, LANES)
            for l in range(LEV):
                xl = x[l]
                across = xl * coef[3]
                for offset in (-3, -2, -1, 1, 2, 3):
                    across += pltpu.roll(xl, (-offset) % SUB, 0) * coef[offset + 3]
                st[l, i, :, span] = xl - 0.08 * (
                    vel[0, l, i, :, span] * along[l] + vel[1, l, i, :, span] * across
                )
        return carry

    def heat(i, carry):
        wet = msk[i].astype(F32)
        rate = 0.5 * (1.0 + jnp.abs(vel[0, LEV - 1, i] - cpl[1, i])) * wet
        st[LEV - 1, i] = st[LEV - 1, i] + rate * (cpl[0, i] - u[LEV - 1, i])
        return carry

    def pack(values, slot, with_mask):
        def body(i, carry):
            packed_w = jnp.zeros((SUB, LANES), F32)
            packed_e = jnp.zeros((SUB, LANES), F32)
            for l in range(LEV + with_mask):
                if l < LEV:
                    left = values[l, i, :, 0:1]
                    right = values[l, i, :, COLS - 1:COLS]
                else:
                    left = msk[i, :, 0:1].astype(F32)
                    right = msk[i, :, COLS - 1:COLS].astype(F32)
                here = lane == l
                packed_w = jnp.where(here, jnp.broadcast_to(left, (SUB, LANES)), packed_w)
                packed_e = jnp.where(here, jnp.broadcast_to(right, (SUB, LANES)), packed_e)
            pack_w[slot, i] = packed_w
            pack_e[slot, i] = packed_e
            return carry

        lax.fori_loop(0, TILES, body, 0)
        for half in range(2):
            for j in range(GROUPS):
                span = slice(j * LANES, (j + 1) * LANES)
                rows = []
                for s in range(8):
                    l = half * 8 + s
                    if l < LEV:
                        rows.append(values[l, TILES - 1, 7:8, span])
                    elif l == LEV:
                        rows.append(msk[TILES - 1, 7:8, span].astype(F32))
                    else:
                        rows.append(jnp.zeros((1, LANES), F32))
                block = jnp.concatenate(rows, axis=0)
                to = GROUPS - 1 - j
                top[slot, half * 8:half * 8 + 8, to * LANES:(to + 1) * LANES] = jnp.take_along_axis(
                    block, flip, axis=1
                )

    def halo_copies(slot):
        base = slot * 5
        copies = [
            remote(pack_w.at[slot], halo_e.at[slot], xs.at[base], xr.at[base], (comp, west)),
            remote(pack_e.at[slot], halo_w.at[slot], xs.at[base + 1], xr.at[base + 1], (comp, east)),
            remote(top.at[slot], mirror.at[slot], xs.at[base + 2], xr.at[base + 2], (comp, fold)),
        ]
        corner_1 = remote(
            top.at[slot, :, pl.ds(0, LANES)], corner_e.at[slot],
            xs.at[base + 3], xr.at[base + 3], (comp, fold_lo),
        )
        corner_2 = remote(
            top.at[slot, :, pl.ds(COLS - LANES, LANES)], corner_w.at[slot],
            xs.at[base + 4], xr.at[base + 4], (comp, fold_hi),
        )
        return copies, corner_1, corner_2

    def exchange_start(slot):
        copies, corner_1, corner_2 = halo_copies(slot)
        for copy in copies:
            copy.start()

        @pl.when(fold_lo != tile)
        def _():
            corner_1.start()

        @pl.when(fold_hi != tile)
        def _():
            corner_2.start()

        @pl.when(fold_lo == tile)
        def _():
            corner_e[slot] = top[slot, :, 0:LANES]

        @pl.when(fold_hi == tile)
        def _():
            corner_w[slot] = top[slot, :, COLS - LANES:COLS]

    def exchange_wait(slot):
        copies, corner_1, corner_2 = halo_copies(slot)
        for copy in copies:
            copy.wait()

        @pl.when(fold_lo != tile)
        def _():
            corner_1.wait()

        @pl.when(fold_hi != tile)
        def _():
            corner_2.wait()

    def beside(x, lanes, left, right):
        from_east = jnp.where(lanes == COLS - 1, right, pltpu.roll(x, COLS - 1, 1))
        from_west = jnp.where(lanes == 0, left, pltpu.roll(x, 1, 1))
        return from_east, from_west

    def column_mean(x, lanes, left, right):
        from_east, from_west = beside(x, lanes, left, right)
        phase = lanes & 3
        near = jnp.where(phase == 3, from_east, from_west)
        return jnp.where((phase == 3) | (phase == 0), 0.5 * (x + near), x)

    def assemble_columns(slot):
        def body(i, carry):
            right_all = halo_e[slot, i]
            left_all = halo_w[slot, i]
            for l in range(LEV):
                right = jnp.broadcast_to(right_all[:, l:l + 1], (SUB, COLS))
                left = jnp.broadcast_to(left_all[:, l:l + 1], (SUB, COLS))
                st[l, i] = column_mean(st[l, i], lane_w, left, right)
            return carry

        lax.fori_loop(0, TILES, body, 0)
        for half in range(2):
            rows = slice(half * 8, half * 8 + 8)
            right = jnp.broadcast_to(corner_e[slot, rows, 0:1], (SUB, COLS))
            left = jnp.broadcast_to(corner_w[slot, rows, LANES - 1:LANES], (SUB, COLS))
            mirror[slot, rows, :] = column_mean(mirror[slot, rows, :], lane_w, left, right)

    def above_below(values, slot, l, i, x):
        is_last = i == TILES - 1
        is_first = i == 0
        nxt = jnp.where(
            is_last, mirror[slot, l:l + 1, :], values[l, jnp.minimum(i + 1, TILES - 1), 0:1, :]
        )
        prev = jnp.where(is_first, x[0:1], values[l, jnp.maximum(i - 1, 0), 7:8, :])
        upper = jnp.where(row_w == 7, jnp.broadcast_to(nxt, (SUB, COLS)), pltpu.roll(x, 7, 0))
        lower = jnp.where(row_w == 0, jnp.broadcast_to(prev, (SUB, COLS)), pltpu.roll(x, 1, 0))
        return upper, lower

    def solve(i, l, value, carried):
        if l > 0:
            value = value + kap[l - 1, i] * carried
        return value * inv[l, i]

    def back_substitute(i, partial):
        result = partial[LEV - 1]
        u[LEV - 1, i] = result
        for l in range(LEV - 2, -1, -1):
            result = partial[l] + inv[l, i] * kap[l, i] * result
            u[l, i] = result

    def assemble_mix(slot):
        def body(i, carry):
            partial = []
            carried = None
            for l in range(LEV):
                x = st[l, i]
                upper, lower = above_below(st, slot, l, i, x)
                near = jnp.where(phase_row == 3, upper, lower)
                x = jnp.where((phase_row == 3) | (phase_row == 0), 0.5 * (x + near), x)
                carried = solve(i, l, x, carried)
                partial.append(carried)
            back_substitute(i, partial)
            return carry

        lax.fori_loop(0, TILES, body, 0)

    def ocean_masks(i):
        wet = msk[i].astype(F32)
        right = jnp.broadcast_to(halo_e[0, i][:, LEV:LEV + 1], (SUB, COLS))
        left = jnp.broadcast_to(halo_w[0, i][:, LEV:LEV + 1], (SUB, COLS))
        m_e, m_w = beside(wet, lane_w, left, right)
        nxt = jnp.where(
            i == TILES - 1, mirror[0, LEV:LEV + 1, :],
            msk[jnp.minimum(i + 1, TILES - 1), 0:1, :].astype(F32),
        )
        prev = jnp.where(i == 0, 0.0, msk[jnp.maximum(i - 1, 0), 7:8, :].astype(F32))
        m_n = jnp.where(row_w == 7, jnp.broadcast_to(nxt, (SUB, COLS)), pltpu.roll(wet, 7, 0))
        m_s = jnp.where(row_w == 0, jnp.broadcast_to(prev, (SUB, COLS)), pltpu.roll(wet, 1, 0))
        return wet * m_e, wet * m_w, wet * m_n, wet * m_s

    def ocean_tendency(values, slot, l, i, masks):
        a = values[l, i]
        right = jnp.broadcast_to(halo_e[slot, i, :, l:l + 1], (SUB, COLS))
        left = jnp.broadcast_to(halo_w[slot, i, :, l:l + 1], (SUB, COLS))
        e, w = beside(a, lane_w, left, right)
        n, s = above_below(values, slot, l, i, a)
        d_e = masks[0] * (e - a)
        d_w = masks[1] * (w - a)
        d_n = masks[2] * (n - a)
        d_s = masks[3] * (s - a)
        return 0.15 * (d_e + d_w + d_n + d_s) - 0.25 * (
            vel[0, l, i] * (d_e - d_w) + vel[1, l, i] * (d_n - d_s)
        )

    def forcing_at(i):
        wet = msk[i].astype(F32)
        return 0.5 * (1.0 + jnp.abs(cpl[1, i] - vel[0, 0, i])) * (cpl[0, i] - u[0, i]) * wet

    lax.fori_loop(0, 2 * BLOCKS // 8, positions, 0)
    for load in loads[2:5]:
        load.wait()

    @pl.when(jnp.logical_not(is_atmos))
    def _():
        pack(u, 0, 1)
        exchange_start(0)

    lax.fori_loop(0, TILES, factors, 0)
    loads[5].wait()

    @pl.when(is_atmos)
    def _():
        lax.fori_loop(0, TILES, tendency, 0)

    @pl.when(jnp.logical_not(is_atmos))
    def _():
        exchange_wait(0)

        def body(i, carry):
            masks = ocean_masks(i)
            for l in range(LEV):
                change = ocean_tendency(u, 0, l, i, masks)
                first[l, i] = change
                st[l, i] = u[l, i] + change
            return carry

        lax.fori_loop(0, TILES, body, 0)

    for send in sends:
        send.wait()
    for slot in range(3):
        for f in range(2):
            win[f, slot * BLOCKS:(slot + 1) * BLOCKS, :] = (
                winb[slot, f].reshape(BLOCKS, LANES).astype(F32)
            )

    for j in order:
        wloads[j].wait()

        def regrid(b, carry):
            for s in range(8):
                block = (b * 8 + s) * GROUPS + j
                sides = []
                for k in range(2):
                    p = pos[block * 2 + k]
                    rows = [win[0, pl.ds(p, 1), :], win[1, pl.ds(p, 1), :]]
                    sides.append(jnp.concatenate(rows + rows[:1] * 6, axis=0))
                picked = jnp.concatenate(sides, axis=1).astype(BF16)
                tiles = jnp.concatenate([wbuf[j, b, s, 0], wbuf[j, b, s, 1]], axis=1)
                result = lax.dot_general(
                    picked, tiles, (((1,), (1,)), ((), ())), preferred_element_type=F32
                )
                cpl[0, b, s:s + 1, j * LANES:(j + 1) * LANES] = result[0:1]
                cpl[1, b, s:s + 1, j * LANES:(j + 1) * LANES] = result[1:2]
            return carry

        lax.fori_loop(0, TILES, regrid, 0, unroll=4)

    cpl_copy = local(cpl, cpl_out, osem.at[0])
    cpl_copy.start()

    @pl.when(is_atmos)
    def _():
        for step in range(2):
            if step == 1:
                lax.fori_loop(0, TILES, tendency, 0)
            lax.fori_loop(0, TILES, heat, 0)
            pack(st, step, 0)
            exchange_start(step)
            exchange_wait(step)
            assemble_columns(step)
            assemble_mix(step)

    @pl.when(jnp.logical_not(is_atmos))
    def _():
        def add_forcing(i, carry):
            st[0, i] = st[0, i] + forcing_at(i)
            return carry

        lax.fori_loop(0, TILES, add_forcing, 0)
        pack(st, 1, 0)
        exchange_start(1)
        exchange_wait(1)

        def body(i, carry):
            masks = ocean_masks(i)
            force = forcing_at(i)
            partial = []
            carried = None
            for l in range(LEV):
                change = ocean_tendency(st, 1, l, i, masks)
                value = u[l, i] + 0.5 * (first[l, i] + change)
                if l == 0:
                    value = value + force
                carried = solve(i, l, value, carried)
                partial.append(carried)
            back_substitute(i, partial)
            return carry

        lax.fori_loop(0, TILES, body, 0)

    adv_copy = local(u, adv_out, osem.at[1])
    adv_copy.start()
    cpl_copy.wait()
    adv_copy.wait()


def on_device(fields, velocity, mixing, surface_mask, intersection_ids, intersection_weights):
    vmem = pl.BlockSpec(memory_space=pltpu.VMEM)
    smem = pl.BlockSpec(memory_space=pltpu.SMEM)
    hbm = pl.BlockSpec(memory_space=pl.ANY)
    scratch = [
        pltpu.VMEM((LEV, TILES, SUB, COLS), F32),
        pltpu.VMEM((2, LEV, TILES, SUB, COLS), F32),
        pltpu.VMEM((LEV - 1, TILES, SUB, COLS), F32),
        pltpu.VMEM((TILES, SUB, COLS), jnp.int32),
        pltpu.VMEM((GROUPS, TILES, SUB, 2, LANES, LANES), BF16),
        pltpu.VMEM((2, TILES, SUB, COLS), F32),
        pltpu.VMEM((2, GROUPS, 64, LANES), BF16),
        pltpu.VMEM((3, 2, GROUPS, 64, LANES), BF16),
        pltpu.VMEM((2, 3 * BLOCKS, LANES), F32),
        pltpu.VMEM((2, TILES, SUB, COLS), F32),
        pltpu.VMEM((LEV, TILES, SUB, COLS), F32),
        pltpu.VMEM((LEV, TILES, SUB, COLS), F32),
        pltpu.VMEM((LEV, TILES, SUB, COLS), F32),
        pltpu.SMEM((2 * BLOCKS,), jnp.int32),
        pltpu.VMEM((2, TILES, SUB, LANES), F32),
        pltpu.VMEM((2, TILES, SUB, LANES), F32),
        pltpu.VMEM((2, 16, COLS), F32),
        pltpu.VMEM((2, TILES, SUB, LANES), F32),
        pltpu.VMEM((2, TILES, SUB, LANES), F32),
        pltpu.VMEM((2, 16, COLS), F32),
        pltpu.VMEM((2, 16, LANES), F32),
        pltpu.VMEM((2, 16, LANES), F32),
        pltpu.SemaphoreType.DMA((6,)),
        pltpu.SemaphoreType.DMA((GROUPS,)),
        pltpu.SemaphoreType.DMA((2,)),
        pltpu.SemaphoreType.DMA((3,)),
        pltpu.SemaphoreType.DMA((3,)),
        pltpu.SemaphoreType.DMA((10,)),
        pltpu.SemaphoreType.DMA((10,)),
    ]
    advanced, coupled = pl.pallas_call(
        kernel,
        out_shape=(
            jax.ShapeDtypeStruct((LEV, TILES, SUB, COLS), F32),
            jax.ShapeDtypeStruct((2, TILES, SUB, COLS), F32),
        ),
        in_specs=[smem, vmem, vmem, hbm, hbm, hbm, hbm, hbm],
        out_specs=(hbm, hbm),
        scratch_shapes=scratch,
        compiler_params=pltpu.CompilerParams(
            collective_id=0, has_side_effects=True, vmem_limit_bytes=52 << 20
        ),
    )(
        intersection_ids.reshape(2 * BLOCKS),
        jnp.asarray(across_table()),
        jnp.asarray(along_matrix()),
        fields.reshape(LEV, TILES, SUB, COLS),
        velocity.reshape(2, LEV, TILES, SUB, COLS),
        mixing.reshape(LEV - 1, TILES, SUB, COLS),
        surface_mask.reshape(TILES, SUB, COLS),
        intersection_weights.reshape(TILES, SUB, GROUPS, 2, LANES, LANES),
    )
    return (
        advanced.reshape(1, LEV, TILES * SUB, COLS),
        coupled.reshape(1, 2, TILES * SUB, COLS),
    )


def solution(mesh):
    placed = (
        P("comp", None, None, "tile"),
        P("comp", None, None, None, "tile"),
        P("comp", None, None, "tile"),
        P("comp", None, "tile"),
        P("comp", "tile", None),
        P("comp", "tile", None, None, None),
    )
    return jax.shard_map(
        on_device,
        mesh=mesh,
        in_specs=placed,
        out_specs=(P("comp", None, None, "tile"), P("comp", None, None, "tile")),
        check_vma=False,
    )
```

```python
import functools
import math

import jax
import jax.numpy as jnp
import numpy as np
from jax import lax
from jax.experimental import pallas as pl
from jax.experimental.pallas import tpu as pltpu
from jax.sharding import PartitionSpec as P

LEV = 14
TILES = 8
SUB = 8
COLS = 512
LANES = 128
GROUPS = 4
BLOCKS = 256
N_TILE = 64
MESH = pl.DeviceIdType.MESH
F32 = jnp.float32
BF16 = jnp.bfloat16


def gll_table():
    nodes = [-1.0, -1.0 / math.sqrt(5.0), 1.0 / math.sqrt(5.0), 1.0]
    weights = [math.prod(nodes[i] - nodes[j] for j in range(4) if j != i) for i in range(4)]
    table = np.zeros((4, 4))
    for i in range(4):
        for j in range(4):
            if i == j:
                table[i, j] = sum(1.0 / (nodes[i] - nodes[k]) for k in range(4) if k != i)
            else:
                table[i, j] = weights[i] / weights[j] / (nodes[i] - nodes[j])
    return table


def along_matrix():
    full = np.kron(np.eye(LANES // 4), gll_table().T).astype(np.float32)
    return full


def across_table():
    table = gll_table()
    coefs = np.zeros((4, SUB, LANES), np.float32)
    for row in range(SUB):
        for m in range(4):
            coefs[m, row, :] = table[row % 4, m]
    return coefs


def kernel(
    ids_in, coef_in, deriv_in, fields, velocity, mixing, mask_in, weights,
    u, cpl,
    vel, kap, msk, wbuf, surf, src, winb, win, st, work, inv,
    ids, pos_v, pos, coef, deriv, dmat, pack, top, halo_e, halo_w, mirror,
    delta, delta_out, delta_in, delta_side,
    lsem, wsem, e0s, e0r, xs, xr,
):
    comp = lax.axis_index("comp")
    tile = lax.axis_index("tile")
    other = 1 - comp
    east = lax.rem(tile + 1, N_TILE)
    west = lax.rem(tile + N_TILE - 1, N_TILE)
    fold = N_TILE - 1 - tile
    fold_lo = lax.rem(fold + N_TILE - 1, N_TILE)
    fold_hi = lax.rem(fold + 1, N_TILE)
    is_atmos = comp == 0
    is_ocean = comp == 1
    level_s = jnp.where(is_atmos, LEV - 1, 0)
    spans = [slice(j * LANES, (j + 1) * LANES) for j in range(GROUPS)]

    def local(src_ref, dst_ref, sem):
        return pltpu.make_async_copy(src_ref, dst_ref, sem)

    def remote(src_ref, dst_ref, send, recv, target):
        return pltpu.make_async_remote_copy(
            src_ref=src_ref, dst_ref=dst_ref, send_sem=send, recv_sem=recv,
            device_id=target, device_id_type=MESH,
        )

    loads = [
        local(fields.at[level_s], surf.at[0], lsem.at[0]),
        local(velocity.at[0, level_s], surf.at[1], lsem.at[1]),
        local(fields, u, lsem.at[2]),
        local(mask_in, msk, lsem.at[3]),
        local(mixing, kap, lsem.at[4]),
        local(velocity, vel, lsem.at[5]),
        local(ids_in, ids, lsem.at[6]),
        local(coef_in, coef, lsem.at[7]),
        local(deriv_in, deriv, lsem.at[8]),
    ]
    order = (0, 3, 1, 2)
    wloads = [local(weights.at[:, :, j], wbuf.at[j], wsem.at[j]) for j in range(GROUPS)]
    for load in loads:
        load.start()
    for j in order:
        wloads[j].start()

    barrier = pltpu.get_barrier_semaphore()
    for target in (
        (other, tile), (comp, east), (comp, west), (comp, fold),
    ):
        pl.semaphore_signal(barrier, inc=1, device_id=target, device_id_type=MESH)

    @pl.when(fold_lo != tile)
    def _():
        pl.semaphore_signal(barrier, inc=1, device_id=(comp, fold_lo), device_id_type=MESH)

    @pl.when(fold_hi != tile)
    def _():
        pl.semaphore_signal(barrier, inc=1, device_id=(comp, fold_hi), device_id_type=MESH)

    loads[0].wait()
    loads[1].wait()
    for f in range(2):
        for j in range(GROUPS):
            src[f, j] = surf[f, :, :, spans[j]].reshape(64, LANES).astype(BF16)

    selfs = jnp.where(fold_lo == tile, 1, 0) + jnp.where(fold_hi == tile, 1, 0)
    pl.semaphore_wait(barrier, 6 - selfs)

    center = remote(src, winb.at[1], e0s.at[1], e0r.at[1], (other, tile))
    center.start()
    forwards = [
        remote(winb.at[1], winb.at[0], e0s.at[0], e0r.at[0], (comp, east)),
        remote(winb.at[1], winb.at[2], e0s.at[2], e0r.at[2], (comp, west)),
    ]

    lane = lax.broadcasted_iota(jnp.int32, (SUB, LANES), 1)
    row = lax.broadcasted_iota(jnp.int32, (SUB, LANES), 0)
    lane_w = lax.broadcasted_iota(jnp.int32, (SUB, COLS), 1)
    row_w = lax.broadcasted_iota(jnp.int32, (SUB, COLS), 0)
    flip = (LANES - 1) - lane
    low_half = lane < 64
    pair_lane = jnp.where(
        (lane & 3) == 3, (lane + 1) & (LANES - 1),
        jnp.where((lane & 3) == 0, (lane + LANES - 1) & (LANES - 1), lane),
    )
    pair_row = jnp.where(
        (row & 3) == 3, (row + 1) & 7, jnp.where((row & 3) == 0, (row + 7) & 7, row)
    )
    ends = jnp.where(low_half, 0, LANES - 1)
    element = row & 4

    def lanes_of(x, index):
        return jnp.take_along_axis(x, index, axis=1)

    def rows_of(x, index):
        return jnp.take_along_axis(x, index, axis=0)

    def row_pair_sum(x, following, previous):
        mixed = jnp.where(row == 0, following, jnp.where(row == SUB - 1, previous, x))
        return x + rows_of(mixed, pair_row)

    def column_pair_sum(ys, sides):
        result = []
        for j in range(GROUPS):
            after = ys[j + 1] if j < GROUPS - 1 else sides
            before = ys[j - 1] if j > 0 else sides
            mixed = jnp.where(lane == 0, after, jnp.where(lane == LANES - 1, before, ys[j]))
            result.append(ys[j] + lanes_of(mixed, pair_lane))
        return result

    def factors(i, carry):
        above = None
        ratio = None
        for l in range(LEV):
            diagonal = 1.0
            if l < LEV - 1:
                below = kap[l, i]
                diagonal = below + 1.0
            if l > 0:
                diagonal = diagonal + above * (1.0 - ratio)
            inverse = 1.0 / diagonal
            inv[l, i] = inverse
            if l < LEV - 1:
                ratio = below * inverse
                above = below
        return carry

    def tendency(i, carry):
        for j in range(GROUPS):
            span = spans[j]
            x = u[:, i, :, span]
            flat = x.reshape(LEV * SUB, LANES)
            high = flat.astype(BF16)
            low = (flat - high.astype(F32)).astype(BF16)
            product = jnp.dot(
                jnp.concatenate([high, low], axis=1), dmat[...], preferred_element_type=F32
            )
            along = (product[:, :LANES] + product[:, LANES:]).reshape(LEV, SUB, LANES)
            for l in range(LEV):
                xl = x[l]
                across = rows_of(xl, element) * coef[0]
                for m in range(1, 4):
                    across += rows_of(xl, element + m) * coef[m]
                st[l, i + 1, :, span] = xl - 0.08 * (
                    vel[0, l, i, :, span] * along[l] + vel[1, l, i, :, span] * across
                )
        return carry

    def heat_rate(i, span):
        wet = msk[i, :, span].astype(F32)
        return 0.5 * (1.0 + jnp.abs(surf[1, i, :, span] - cpl[1, i, :, span])) * wet

    def heat(i, carry):
        for span in spans:
            st[LEV - 1, i + 1, :, span] = st[LEV - 1, i + 1, :, span] + heat_rate(i, span) * (
                cpl[0, i, :, span] - u[LEV - 1, i, :, span]
            )
        return carry

    def delta_at(i, span):
        return heat_rate(i, span) * (cpl[0, i, :, span] - surf[0, i, :, span])

    def side_pack(left, right):
        return lanes_of(jnp.where(lane == 0, left, right), ends)

    def pack_edges(values, shift, slot, with_mask):
        def body(i, carry):
            packed = jnp.zeros((SUB, LANES), F32)
            for l in range(LEV + with_mask):
                if l < LEV:
                    left = values[l, i + shift, :, spans[0]]
                    right = values[l, i + shift, :, spans[-1]]
                else:
                    left = msk[i, :, spans[0]].astype(F32)
                    right = msk[i, :, spans[-1]].astype(F32)
                packed = jnp.where((lane & 63) == l, side_pack(left, right), packed)
            pack[slot, i] = packed
            return carry

        lax.fori_loop(0, TILES, body, 0)
        pack[slot, TILES, 0:1, :] = pltpu.roll(pack[slot, TILES - 1], 64, 1)[SUB - 1:SUB]
        for half in range(2):
            for j in range(GROUPS):
                rows = []
                for s in range(8):
                    l = half * 8 + s
                    if l < LEV:
                        rows.append(values[l, TILES - 1 + shift, 7:8, spans[j]])
                    elif l == LEV:
                        rows.append(msk[TILES - 1, 7:8, spans[j]].astype(F32))
                    else:
                        rows.append(jnp.zeros((1, LANES), F32))
                block = jnp.concatenate(rows, axis=0)
                top[slot, half * 8:half * 8 + 8, spans[GROUPS - 1 - j]] = lanes_of(block, flip)

    def exchange(base, to_sides, to_fold, to_corner, at_east, at_west, at_fold, at_lo, at_hi):
        copies = [
            remote(to_sides, at_east, xs.at[base], xr.at[base], (comp, west)),
            remote(to_sides, at_west, xs.at[base + 1], xr.at[base + 1], (comp, east)),
            remote(to_fold, at_fold, xs.at[base + 2], xr.at[base + 2], (comp, fold)),
        ]
        lo = remote(to_corner, at_lo, xs.at[base + 3], xr.at[base + 3], (comp, fold_lo))
        hi = remote(to_corner, at_hi, xs.at[base + 4], xr.at[base + 4], (comp, fold_hi))

        def start():
            for copy in copies:
                copy.start()

            @pl.when(fold_lo != tile)
            def _():
                lo.start()

            @pl.when(fold_hi != tile)
            def _():
                hi.start()

            @pl.when(fold_lo == tile)
            def _():
                at_lo[...] = to_corner[...]

            @pl.when(fold_hi == tile)
            def _():
                at_hi[...] = to_corner[...]

        def wait():
            for copy in copies:
                copy.wait()

            @pl.when(fold_lo != tile)
            def _():
                lo.wait()

            @pl.when(fold_hi != tile)
            def _():
                hi.wait()

        return start, wait

    def halo_exchange(slot):
        inner = pl.ds(0, TILES)
        return exchange(
            slot * 5, pack.at[slot, inner], top.at[slot], pack.at[slot, TILES],
            halo_e.at[slot, pl.ds(1, TILES)], halo_w.at[slot, pl.ds(1, TILES)],
            mirror.at[slot], halo_e.at[slot, TILES + 1], halo_w.at[slot, TILES + 1],
        )

    def delta_exchange():
        return exchange(
            10, delta_out.at[0], delta_out.at[1], delta_out.at[2],
            delta_in.at[0], delta_in.at[1], delta_in.at[2], delta_in.at[3], delta_in.at[4],
        )

    def fill_pads(slot):
        for l in range(LEV):
            st[l, 0, 7:8, :] = st[l, 1, 0:1, :]
            st[l, TILES + 1, 0:1, :] = mirror[slot, l:l + 1, :]
        halo_e[slot, 0, 7:8, :] = halo_e[slot, 1, 0:1, :]
        halo_w[slot, 0, 7:8, :] = halo_w[slot, 1, 0:1, :]

    def side_halo(slot, k):
        return jnp.where(low_half, halo_e[slot, k], halo_w[slot, k])

    def side_pick(halos, l):
        return lanes_of(halos, jnp.where(low_half, l, 64 + l))

    def assembled(slot, l, i, halos):
        ys = [
            row_pair_sum(st[l, i + 1, :, span], st[l, i + 2, :, span], st[l, i, :, span])
            for span in spans
        ]
        sums = column_pair_sum(ys, side_pick(halos, l))
        return [0.25 * value for value in sums]

    def eliminate(i, l, j, value, carried):
        if l > 0:
            value = value + kap[l - 1, i, :, spans[j]] * carried
        return value * inv[l, i, :, spans[j]]

    def back_substitute(i, j, partial):
        span = spans[j]
        result = partial[LEV - 1]
        u[LEV - 1, i, :, span] = result
        for l in range(LEV - 2, -1, -1):
            result = partial[l] + inv[l, i, :, span] * kap[l, i, :, span] * result
            u[l, i, :, span] = result

    def assemble_forward(slot, finish):
        def body(i, carry):
            halos = row_pair_sum(
                side_halo(slot, i + 1), side_halo(slot, i + 2), side_halo(slot, i)
            )
            carried = [None] * GROUPS
            partial = [[] for _ in range(GROUPS)]
            for l in range(LEV):
                values = assembled(slot, l, i, halos)
                for j in range(GROUPS):
                    if finish or l < LEV - 1:
                        carried[j] = eliminate(i, l, j, values[j], carried[j])
                    else:
                        carried[j] = values[j]
                    if finish:
                        partial[j].append(carried[j])
                    else:
                        work[l, i, :, spans[j]] = carried[j]
            if finish:
                for j in range(GROUPS):
                    back_substitute(i, j, partial[j])
            return carry

        lax.fori_loop(0, TILES, body, 0)

    def finish_first(i, carry):
        ys = [
            row_pair_sum(delta[i + 1, :, span], delta[i + 2, :, span], delta[i, :, span])
            for span in spans
        ]
        sums = column_pair_sum(ys, delta_side[i])
        for j in range(GROUPS):
            span = spans[j]
            partial = [work[l, i, :, span] for l in range(LEV - 1)]
            value = work[LEV - 1, i, :, span] + 0.25 * sums[j]
            partial.append(eliminate(i, LEV - 1, j, value, partial[-1]))
            back_substitute(i, j, partial)
        return carry

    def beside(x, left, right):
        from_east = jnp.where(lane_w == COLS - 1, right, pltpu.roll(x, COLS - 1, 1))
        from_west = jnp.where(lane_w == 0, left, pltpu.roll(x, 1, 1))
        return from_east, from_west

    def beyond(x, nxt, prev):
        upper = jnp.where(row_w == 7, jnp.broadcast_to(nxt, (SUB, COLS)), pltpu.roll(x, 7, 0))
        lower = jnp.where(row_w == 0, jnp.broadcast_to(prev, (SUB, COLS)), pltpu.roll(x, 1, 0))
        return upper, lower

    def ocean_sides(slot, i, l):
        right = jnp.broadcast_to(halo_e[slot, i + 1, :, l:l + 1], (SUB, COLS))
        left = jnp.broadcast_to(halo_w[slot, i + 1, :, 64 + l:65 + l], (SUB, COLS))
        return left, right

    def ocean_masks(i):
        wet = msk[i].astype(F32)
        m_e, m_w = beside(wet, *ocean_sides(0, i, LEV))
        nxt = jnp.where(
            i == TILES - 1, mirror[0, LEV:LEV + 1, :],
            msk[jnp.minimum(i + 1, TILES - 1), 0:1, :].astype(F32),
        )
        prev = jnp.where(i == 0, 0.0, msk[jnp.maximum(i - 1, 0), 7:8, :].astype(F32))
        m_n, m_s = beyond(wet, nxt, prev)
        return wet * m_e, wet * m_w, wet * m_n, wet * m_s

    def ocean_change(a, e, w, n, s, l, i, masks):
        d_e = masks[0] * (e - a)
        d_w = masks[1] * (w - a)
        d_n = masks[2] * (n - a)
        d_s = masks[3] * (s - a)
        return 0.15 * (d_e + d_w + d_n + d_s) - 0.25 * (
            vel[0, l, i] * (d_e - d_w) + vel[1, l, i] * (d_n - d_s)
        )

    def ocean_first(i, carry):
        masks = ocean_masks(i)
        for l in range(LEV):
            a = u[l, i]
            nxt = jnp.where(
                i == TILES - 1, mirror[0, l:l + 1, :], u[l, jnp.minimum(i + 1, TILES - 1), 0:1, :]
            )
            prev = jnp.where(i == 0, a[0:1], u[l, jnp.maximum(i - 1, 0), 7:8, :])
            e, w = beside(a, *ocean_sides(0, i, l))
            n, s = beyond(a, nxt, prev)
            change = ocean_change(a, e, w, n, s, l, i, masks)
            work[l, i] = change
            st[l, i + 1] = a + change
        return carry

    def ocean_second(i, carry):
        masks = ocean_masks(i)
        partial = [[] for _ in range(GROUPS)]
        carried = [None] * GROUPS
        for l in range(LEV):
            a = st[l, i + 1]
            e, w = beside(a, *ocean_sides(1, i, l))
            n, s = beyond(a, st[l, i + 2, 0:1, :], st[l, i, 7:8, :])
            change = ocean_change(a, e, w, n, s, l, i, masks)
            value = u[l, i] + 0.5 * (work[l, i] + change)
            if l == 0:
                value = value + delta[i + 1]
            for j in range(GROUPS):
                carried[j] = eliminate(i, l, j, value[:, spans[j]], carried[j])
                partial[j].append(carried[j])
        for j in range(GROUPS):
            back_substitute(i, j, partial[j])
        return carry

    for load in loads[2:9]:
        load.wait()
    high = deriv[...].astype(BF16)
    dmat[0:LANES, 0:LANES] = high
    dmat[0:LANES, LANES:2 * LANES] = (deriv[...] - high.astype(F32)).astype(BF16)
    dmat[LANES:2 * LANES, 0:LANES] = high
    dmat[LANES:2 * LANES, LANES:2 * LANES] = jnp.zeros((LANES, LANES), BF16)

    start_0, wait_0 = halo_exchange(0)
    start_1, wait_1 = halo_exchange(1)
    start_d, wait_d = delta_exchange()

    @pl.when(is_ocean)
    def _():
        pack_edges(u, 0, 0, 1)
        start_0()

    @pl.when(is_atmos)
    def _():
        lax.fori_loop(0, TILES, tendency, 0)
        pack_edges(st, 1, 0, 0)
        start_0()

    lax.fori_loop(0, TILES, factors, 0)

    ident = ids[...]
    relative = (lax.shift_right_logical(ident, 8) - tile + 1 + N_TILE) & (N_TILE - 1)
    block = ident & (BLOCKS - 1)
    pos_v[...] = (
        jnp.minimum(relative, 2) * BLOCKS + (block & 3) * 64 + lax.shift_right_logical(block, 2)
    )
    pos_copy = local(pos_v, pos, lsem.at[9])
    pos_copy.start()

    center.wait()
    for copy in forwards:
        copy.start()
    pos_copy.wait()

    def widen(slot):
        for f in range(2):
            win[f, slot * BLOCKS:(slot + 1) * BLOCKS, :] = (
                winb[slot, f].reshape(BLOCKS, LANES).astype(F32)
            )

    widen(1)
    wait_0()

    @pl.when(is_atmos)
    def _():
        fill_pads(0)
        assemble_forward(0, False)

    @pl.when(is_ocean)
    def _():
        lax.fori_loop(0, TILES, ocean_first, 0)
        pack_edges(st, 1, 1, 0)
        start_1()

    for copy in forwards:
        copy.wait()
    widen(0)
    widen(2)

    def regrid_rows(j, b, rows_in):
        for s in rows_in:
            block = (b * 8 + s) * GROUPS + j
            sides = []
            for k in range(2):
                p = pos[k, block]
                rows = [win[0, pl.ds(p, 1), :], win[1, pl.ds(p, 1), :]]
                sides.append(jnp.concatenate(rows + rows[:1] * 6, axis=0))
            picked = jnp.concatenate(sides, axis=1).astype(BF16)
            tiles = jnp.concatenate([wbuf[j, b, s, 0], wbuf[j, b, s, 1]], axis=1)
            result = lax.dot_general(
                picked, tiles, (((1,), (1,)), ((), ())), preferred_element_type=F32
            )
            cpl[0, b, s:s + 1, spans[j]] = result[0:1]
            cpl[1, b, s:s + 1, spans[j]] = result[1:2]

    def regrid(j):
        def body(b, carry):
            regrid_rows(j, b, range(8))
            return carry

        lax.fori_loop(0, TILES, body, 0, unroll=4)

    for j in order:
        wloads[j].wait()
    regrid(0)
    regrid(3)
    for j in (1, 2):
        regrid_rows(j, TILES - 1, (7,))

    packed = jnp.zeros((SUB, LANES), F32)
    for i in range(TILES):
        packed = jnp.where(
            (lane & 63) == i, side_pack(delta_at(i, spans[0]), delta_at(i, spans[-1])), packed
        )
    delta_out[0] = packed
    rows = [delta_at(TILES - 1, spans[j])[7:8] for j in range(GROUPS - 1, -1, -1)]
    delta_out[1] = lanes_of(jnp.concatenate(rows + rows, axis=0), flip)
    delta_out[2, 0:1, :] = pltpu.roll(packed, 64, 1)[SUB - 1:SUB]
    start_d()
    regrid(1)
    regrid(2)

    def all_delta(i, carry):
        for span in spans:
            delta[i + 1, :, span] = delta_at(i, span)
        return carry

    lax.fori_loop(0, TILES, all_delta, 0)
    wait_d()
    sides = jnp.where(low_half, delta_in[0], delta_in[1])
    for j in range(GROUPS):
        delta[TILES + 1, 0:1, spans[j]] = delta_in[2, j:j + 1, :]
    delta[0, 7:8, :] = delta[1, 0:1, :]

    @pl.when(is_atmos)
    def _():
        corner = jnp.where(low_half, delta_in[3], delta_in[4])
        following = jnp.where((lane & 63) == TILES - 1, corner, pltpu.roll(sides, LANES - 1, 1))
        previous = jnp.where(
            (lane & 63) == 0, jnp.broadcast_to(sides[0:1], (SUB, LANES)), pltpu.roll(sides, 1, 1)
        )
        summed = row_pair_sum(sides, following, previous)
        for i in range(TILES):
            delta_side[i] = side_pick(summed, i)
        lax.fori_loop(0, TILES, finish_first, 0)
        lax.fori_loop(0, TILES, tendency, 0)
        lax.fori_loop(0, TILES, heat, 0)
        pack_edges(st, 1, 1, 0)
        start_1()
        wait_1()
        fill_pads(1)
        assemble_forward(1, True)

    @pl.when(is_ocean)
    def _():
        wait_1()

        def add_forcing(i, carry):
            st[0, i + 1] = st[0, i + 1] + delta[i + 1]
            return carry

        lax.fori_loop(0, TILES, add_forcing, 0)
        mirror[1, 0:1, :] = mirror[1, 0:1, :] + delta[TILES + 1, 0:1, :]
        fill_pads(1)
        for i in range(TILES):
            side = side_pick(sides, i)
            halo_e[1, i + 1] = halo_e[1, i + 1] + jnp.where(lane == 0, side, 0.0)
            halo_w[1, i + 1] = halo_w[1, i + 1] + jnp.where(lane == 64, side, 0.0)
        lax.fori_loop(0, TILES, ocean_second, 0)


def on_device(fields, velocity, mixing, surface_mask, intersection_ids, intersection_weights):
    vmem = pl.BlockSpec(memory_space=pltpu.VMEM)
    hbm = pl.BlockSpec(memory_space=pltpu.HBM)
    scratch = [
        pltpu.VMEM((2, LEV, TILES, SUB, COLS), F32),
        pltpu.VMEM((LEV - 1, TILES, SUB, COLS), F32),
        pltpu.VMEM((TILES, SUB, COLS), jnp.int32),
        pltpu.VMEM((GROUPS, TILES, SUB, 2, LANES, LANES), BF16),
        pltpu.VMEM((2, TILES, SUB, COLS), F32),
        pltpu.VMEM((2, GROUPS, 64, LANES), BF16),
        pltpu.VMEM((3, 2, GROUPS, 64, LANES), BF16),
        pltpu.VMEM((2, 3 * BLOCKS, LANES), F32),
        pltpu.VMEM((LEV, TILES + 2, SUB, COLS), F32),
        pltpu.VMEM((LEV, TILES, SUB, COLS), F32),
        pltpu.VMEM((LEV, TILES, SUB, COLS), F32),
        pltpu.VMEM((2, BLOCKS), jnp.int32),
        pltpu.VMEM((2, BLOCKS), jnp.int32),
        pltpu.SMEM((2, BLOCKS), jnp.int32),
        pltpu.VMEM((4, SUB, LANES), F32),
        pltpu.VMEM((LANES, LANES), F32),
        pltpu.VMEM((2 * LANES, 2 * LANES), BF16),
        pltpu.VMEM((2, TILES + 1, SUB, LANES), F32),
        pltpu.VMEM((2, 16, COLS), F32),
        pltpu.VMEM((2, TILES + 2, SUB, LANES), F32),
        pltpu.VMEM((2, TILES + 2, SUB, LANES), F32),
        pltpu.VMEM((2, 16, COLS), F32),
        pltpu.VMEM((TILES + 2, SUB, COLS), F32),
        pltpu.VMEM((3, SUB, LANES), F32),
        pltpu.VMEM((5, SUB, LANES), F32),
        pltpu.VMEM((TILES, SUB, LANES), F32),
        pltpu.SemaphoreType.DMA((10,)),
        pltpu.SemaphoreType.DMA((GROUPS,)),
        pltpu.SemaphoreType.DMA((3,)),
        pltpu.SemaphoreType.DMA((3,)),
        pltpu.SemaphoreType.DMA((15,)),
        pltpu.SemaphoreType.DMA((15,)),
    ]
    advanced, coupled = pl.pallas_call(
        kernel,
        out_shape=(
            pltpu.VMEM((LEV, TILES, SUB, COLS), F32),
            pltpu.VMEM((2, TILES, SUB, COLS), F32),
        ),
        in_specs=[hbm] * 8,
        out_specs=(vmem, vmem),
        scratch_shapes=scratch,
        compiler_params=pltpu.CompilerParams(
            collective_id=0, has_side_effects=True, vmem_limit_bytes=52 << 20
        ),
    )(
        jnp.transpose(intersection_ids[0], (1, 0)),
        jnp.asarray(across_table()),
        jnp.asarray(along_matrix()),
        fields.reshape(LEV, TILES, SUB, COLS),
        velocity.reshape(2, LEV, TILES, SUB, COLS),
        mixing.reshape(LEV - 1, TILES, SUB, COLS),
        surface_mask.reshape(TILES, SUB, COLS),
        intersection_weights.reshape(TILES, SUB, GROUPS, 2, LANES, LANES),
    )
    return (
        advanced.reshape(1, LEV, TILES * SUB, COLS),
        coupled.reshape(1, 2, TILES * SUB, COLS),
    )


def solution(mesh):
    placed = (
        P("comp", None, None, "tile"),
        P("comp", None, None, None, "tile"),
        P("comp", None, None, "tile"),
        P("comp", None, "tile"),
        P("comp", "tile", None),
        P("comp", "tile", None, None, None),
    )
    return jax.shard_map(
        on_device,
        mesh=mesh,
        in_specs=placed,
        out_specs=(P("comp", None, None, "tile"), P("comp", None, None, "tile")),
        check_vma=False,
    )
```

```python
import functools
import math

import jax
import jax.numpy as jnp
import numpy as np
from jax import lax
from jax.experimental import pallas as pl
from jax.experimental.pallas import tpu as pltpu
from jax.sharding import PartitionSpec as P

LEV = 14
TILES = 8
SUB = 8
COLS = 512
LANES = 128
GROUPS = 4
BLOCKS = 256
N_TILE = 64
MESH = pl.DeviceIdType.MESH
F32 = jnp.float32
BF16 = jnp.bfloat16


def gll_table():
    nodes = [-1.0, -1.0 / math.sqrt(5.0), 1.0 / math.sqrt(5.0), 1.0]
    weights = [math.prod(nodes[i] - nodes[j] for j in range(4) if j != i) for i in range(4)]
    table = np.zeros((4, 4))
    for i in range(4):
        for j in range(4):
            if i == j:
                table[i, j] = sum(1.0 / (nodes[i] - nodes[k]) for k in range(4) if k != i)
            else:
                table[i, j] = weights[i] / weights[j] / (nodes[i] - nodes[j])
    return table


def along_matrix():
    full = np.kron(np.eye(LANES // 4), gll_table().T).astype(np.float32)
    return full


def across_table():
    table = gll_table()
    coefs = np.zeros((4, SUB, LANES), np.float32)
    for row in range(SUB):
        for m in range(4):
            coefs[m, row, :] = table[row % 4, m]
    return coefs


def kernel(
    ids_in, coef_in, deriv_in, fields, velocity, mixing, mask_in, weights,
    u, cpl,
    vel, kap, elim, msk, wbuf, surf, src, winb, win, st, work, inv,
    ids, pos_v, pos, coef, deriv, dmat, pack, dense, top, halo, sides_at, mirror,
    delta, delta_out, delta_in, delta_side,
    lsem, wsem, e0s, e0r, xs, xr,
):
    comp = lax.axis_index("comp")
    tile = lax.axis_index("tile")
    other = 1 - comp
    east = lax.rem(tile + 1, N_TILE)
    west = lax.rem(tile + N_TILE - 1, N_TILE)
    fold = N_TILE - 1 - tile
    fold_lo = lax.rem(fold + N_TILE - 1, N_TILE)
    fold_hi = lax.rem(fold + 1, N_TILE)
    is_atmos = comp == 0
    is_ocean = comp == 1
    level_s = jnp.where(is_atmos, LEV - 1, 0)
    spans = [slice(j * LANES, (j + 1) * LANES) for j in range(GROUPS)]

    def local(src_ref, dst_ref, sem):
        return pltpu.make_async_copy(src_ref, dst_ref, sem)

    def remote(src_ref, dst_ref, send, recv, target):
        return pltpu.make_async_remote_copy(
            src_ref=src_ref, dst_ref=dst_ref, send_sem=send, recv_sem=recv,
            device_id=target, device_id_type=MESH,
        )

    loads = [
        local(fields.at[level_s], surf.at[0], lsem.at[0]),
        local(velocity.at[0, level_s], surf.at[1], lsem.at[1]),
        local(fields, u, lsem.at[2]),
        local(mask_in, msk, lsem.at[3]),
        local(mixing, kap, lsem.at[4]),
        local(velocity, vel, lsem.at[5]),
        local(ids_in, ids, lsem.at[6]),
        local(coef_in, coef, lsem.at[7]),
        local(deriv_in, deriv, lsem.at[8]),
    ]
    order = (0, 3, 1, 2)
    wloads = [local(weights.at[:, :, j], wbuf.at[j], wsem.at[j]) for j in range(GROUPS)]
    for load in loads:
        load.start()

    for j in order:
        wloads[j].start()

    barrier = pltpu.get_barrier_semaphore()
    for target in (
        (other, tile), (comp, east), (comp, west), (comp, fold),
    ):
        pl.semaphore_signal(barrier, inc=1, device_id=target, device_id_type=MESH)

    @pl.when(fold_lo != tile)
    def _():
        pl.semaphore_signal(barrier, inc=1, device_id=(comp, fold_lo), device_id_type=MESH)

    @pl.when(fold_hi != tile)
    def _():
        pl.semaphore_signal(barrier, inc=1, device_id=(comp, fold_hi), device_id_type=MESH)

    loads[0].wait()
    loads[1].wait()
    for f in range(2):
        for j in range(GROUPS):
            src[f, j] = surf[f, :, :, spans[j]].reshape(64, LANES).astype(BF16)

    selfs = jnp.where(fold_lo == tile, 1, 0) + jnp.where(fold_hi == tile, 1, 0)
    pl.semaphore_wait(barrier, 6 - selfs)

    center = remote(src, winb.at[1], e0s.at[1], e0r.at[1], (other, tile))
    center.start()
    forwards = [
        remote(winb.at[1], winb.at[0], e0s.at[0], e0r.at[0], (comp, east)),
        remote(winb.at[1], winb.at[2], e0s.at[2], e0r.at[2], (comp, west)),
    ]

    lane = lax.broadcasted_iota(jnp.int32, (SUB, LANES), 1)
    row = lax.broadcasted_iota(jnp.int32, (SUB, LANES), 0)
    lane_w = lax.broadcasted_iota(jnp.int32, (SUB, COLS), 1)
    row_w = lax.broadcasted_iota(jnp.int32, (SUB, COLS), 0)
    flip = (LANES - 1) - lane
    low_half = lane < 64
    pair_lane = jnp.where(
        (lane & 3) == 3, (lane + 1) & (LANES - 1),
        jnp.where((lane & 3) == 0, (lane + LANES - 1) & (LANES - 1), lane),
    )
    pair_row = jnp.where(
        (row & 3) == 3, (row + 1) & 7, jnp.where((row & 3) == 0, (row + 7) & 7, row)
    )
    ends = jnp.where(low_half, 0, LANES - 1)
    element = row & 4

    def lanes_of(x, index):
        return jnp.take_along_axis(x, index, axis=1)

    def rows_of(x, index):
        return jnp.take_along_axis(x, index, axis=0)

    def row_pair_sum(x, following, previous):
        mixed = jnp.where(row == 0, following, jnp.where(row == SUB - 1, previous, x))
        return x + rows_of(mixed, pair_row)

    def column_pair_sum(ys, sides, groups=range(GROUPS)):
        result = {}
        for j in groups:
            after = ys[j + 1] if j < GROUPS - 1 else sides
            before = ys[j - 1] if j > 0 else sides
            mixed = jnp.where(lane == 0, after, jnp.where(lane == LANES - 1, before, ys[j]))
            result[j] = ys[j] + lanes_of(mixed, pair_lane)
        return result

    def factors(i, carry):
        above = None
        ratio = None
        for l in range(LEV):
            diagonal = 1.0
            if l < LEV - 1:
                below = kap[l, i]
                diagonal = below + 1.0
            if l > 0:
                diagonal = diagonal + above * (1.0 - ratio)
            inverse = 1.0 / diagonal
            inv[l, i] = inverse
            if l > 0:
                elim[l - 1, i] = above * inverse
            if l < LEV - 1:
                ratio = below * inverse
                above = below
                kap[l, i] = ratio
        return carry

    def tendency(units, heated):
        xs = [u[:, i, :, spans[j]] for i, j in units]
        flat = jnp.concatenate([x.reshape(LEV * SUB, LANES) for x in xs], axis=0)
        high = flat.astype(BF16)
        low = (flat - high.astype(F32)).astype(BF16)
        product = jnp.dot(
            jnp.concatenate([high, low], axis=1), dmat[...], preferred_element_type=F32
        )
        for n, (i, j) in enumerate(units):
            span = spans[j]
            part = product[n * LEV * SUB:(n + 1) * LEV * SUB]
            along = (part[:, :LANES] + part[:, LANES:]).reshape(LEV, SUB, LANES)
            for l in range(LEV):
                xl = xs[n][l]
                across = rows_of(xl, element) * coef[0]
                for m in range(1, 4):
                    across += rows_of(xl, element + m) * coef[m]
                value = xl - 0.08 * (
                    vel[0, l, i, :, span] * along[l] + vel[1, l, i, :, span] * across
                )
                if heated and l == LEV - 1:
                    value = value + heat_rate(i, span) * (cpl[0, i, :, span] - xl)
                st[l, i + 1, :, span] = value

    def heat_rate(i, span):
        wet = msk[i, :, span].astype(F32)
        return 0.5 * (1.0 + jnp.abs(surf[1, i, :, span] - cpl[1, i, :, span])) * wet

    def delta_at(i, span):
        return heat_rate(i, span) * (cpl[0, i, :, span] - surf[0, i, :, span])

    def turned(x, amount):
        amount = amount % LANES
        return x if amount == 0 else pltpu.roll(x, amount, 1)

    def side_pack(left, right):
        return lanes_of(jnp.where(lane == 0, left, right), ends)

    def pack_edges(values, shift, slot, with_mask):
        def body(i, carry):
            packed = jnp.zeros((SUB, LANES), F32)
            for l in range(LEV + with_mask):
                if l < LEV:
                    left = values[l, i + shift, :, spans[0]]
                    right = values[l, i + shift, :, spans[-1]]
                else:
                    left = msk[i, :, spans[0]].astype(F32)
                    right = msk[i, :, spans[-1]].astype(F32)
                packed = jnp.where((lane & 63) == l, side_pack(left, right), packed)
            pack[i] = packed
            return carry

        lax.fori_loop(0, TILES, body, 0, unroll=8)
        dense_w = jnp.zeros((SUB, LANES), F32)
        dense_e = jnp.zeros((SUB, LANES), F32)
        for i in range(TILES):
            here = lax.shift_right_logical(lane, 4) == i
            dense_w = jnp.where(here, turned(pack[i], 16 * i), dense_w)
            dense_e = jnp.where(here, turned(pack[i], 16 * i - 64), dense_e)
        dense[slot, 0] = dense_w
        dense[slot, 1] = dense_e
        for half in range(2):
            for j in range(GROUPS):
                rows = []
                for s in range(8):
                    l = half * 8 + s
                    if l < LEV:
                        rows.append(values[l, TILES - 1 + shift, 7:8, spans[j]])
                    elif l == LEV:
                        rows.append(msk[TILES - 1, 7:8, spans[j]].astype(F32))
                    else:
                        rows.append(jnp.zeros((1, LANES), F32))
                block = jnp.concatenate(rows, axis=0)
                top[slot, half * 8:half * 8 + 8, spans[GROUPS - 1 - j]] = lanes_of(block, flip)

    def exchange(base, to_west, to_east, to_fold, to_lo, to_hi, at):
        copies = [
            remote(to_fold, at[2], xs.at[base + 2], xr.at[base + 2], (comp, fold)),
            remote(to_west, at[0], xs.at[base], xr.at[base], (comp, west)),
            remote(to_east, at[1], xs.at[base + 1], xr.at[base + 1], (comp, east)),
        ]
        lo = remote(to_lo, at[3], xs.at[base + 3], xr.at[base + 3], (comp, fold_lo))
        hi = remote(to_hi, at[4], xs.at[base + 4], xr.at[base + 4], (comp, fold_hi))

        def start():
            for copy in copies:
                copy.start()

            @pl.when(fold_lo != tile)
            def _():
                lo.start()

            @pl.when(fold_hi != tile)
            def _():
                hi.start()

            @pl.when(fold_lo == tile)
            def _():
                at[3][...] = to_lo[...]

            @pl.when(fold_hi == tile)
            def _():
                at[4][...] = to_hi[...]

        def wait():
            for copy in copies:
                copy.wait_recv()

            @pl.when(fold_lo != tile)
            def _():
                lo.wait_recv()

            @pl.when(fold_hi != tile)
            def _():
                hi.wait_recv()

        def drain():
            for copy in copies:
                copy.wait_send()

            @pl.when(fold_lo != tile)
            def _():
                lo.wait_send()

            @pl.when(fold_hi != tile)
            def _():
                hi.wait_send()

        return start, wait, drain

    def halo_exchange(slot):
        return exchange(
            slot * 5, dense.at[slot, 0], dense.at[slot, 1], top.at[slot],
            dense.at[slot, 1], dense.at[slot, 0],
            [halo.at[slot, 0], halo.at[slot, 1], mirror.at[slot], halo.at[slot, 2], halo.at[slot, 3]],
        )

    def delta_exchange():
        return exchange(
            10, delta_out.at[0], delta_out.at[0], delta_out.at[1], delta_out.at[2], delta_out.at[2],
            [delta_in.at[n] for n in range(5)],
        )

    def fill_south():
        for l in range(LEV):
            st[l, 0, 7:8, :] = st[l, 1, 0:1, :]

    def fill_north(slot):
        for l in range(LEV):
            st[l, TILES + 1, 0:1, :] = mirror[slot, l:l + 1, :]

    def spread_sides(slot, summed):
        both = []
        for n in range(2):
            h = halo[slot, n]
            if summed:
                corner = pltpu.roll(halo[slot, 2 + n], 1, 0)
                following = jnp.where(lane >= LANES - 16, corner, turned(h, -16))
                previous = jnp.where(
                    lane < 16, jnp.broadcast_to(h[0:1], (SUB, LANES)), turned(h, 16)
                )
                h = row_pair_sum(h, following, previous)
            both.append(h)
        for i in range(TILES):
            sides_at[slot, i] = jnp.where(
                low_half, turned(both[0], -16 * i), turned(both[1], 64 - 16 * i)
            )

    def side_pick(halos, l):
        return lanes_of(halos, jnp.where(low_half, l, 64 + l))

    def row_sums(l, i):
        return [
            row_pair_sum(st[l, i + 1, :, span], st[l, i + 2, :, span], st[l, i, :, span])
            for span in spans
        ]

    def eliminate(i, l, j, value, carried):
        value = value * inv[l, i, :, spans[j]]
        if l > 0:
            value = value + elim[l - 1, i, :, spans[j]] * carried
        return value

    def back_substitute(i, j, partial):
        span = spans[j]
        result = partial[LEV - 1]
        u[LEV - 1, i, :, span] = result
        for l in range(LEV - 2, -1, -1):
            result = partial[l] + kap[l, i, :, span] * result
            u[l, i, :, span] = result

    def forward_first(i, carry):
        halos = sides_at[0, i]
        carried = [None] * GROUPS
        for l in range(LEV):
            sums = column_pair_sum(row_sums(l, i), side_pick(halos, l))
            for j in range(GROUPS):
                carried[j] = 0.25 * sums[j]
                if l < LEV - 1:
                    carried[j] = eliminate(i, l, j, carried[j], previous[j] if l else None)
                work[l, i, :, spans[j]] = carried[j]
            previous = list(carried)
        return carry

    def finish_first(i, groups):
        ys = [
            row_pair_sum(delta[i + 1, :, span], delta[i + 2, :, span], delta[i, :, span])
            for span in spans
        ]
        sums = column_pair_sum(ys, delta_side[i], groups)
        for j in groups:
            span = spans[j]
            partial = [work[l, i, :, span] for l in range(LEV - 1)]
            value = work[LEV - 1, i, :, span] + 0.25 * sums[j]
            partial.append(eliminate(i, LEV - 1, j, value, partial[-1]))
            back_substitute(i, j, partial)

    def finish_second(i, groups, ys_at, halos):
        carried = {j: None for j in groups}
        partial = {j: [] for j in groups}
        for l in range(LEV):
            sides = halos if halos is None else side_pick(halos, l)
            sums = column_pair_sum(ys_at(l), sides, groups)
            for j in groups:
                carried[j] = eliminate(i, l, j, 0.25 * sums[j], carried[j])
                partial[j].append(carried[j])
        for j in groups:
            back_substitute(i, j, partial[j])

    def second_middle(i, carry):
        def ys_at(l):
            ys = row_sums(l, i)
            for j in range(GROUPS):
                work[l, i, :, spans[j]] = ys[j]
            return ys

        finish_second(i, (1, 2), ys_at, None)
        return carry

    def second_sides(i, carry):
        def ys_at(l):
            return [work[l, i, :, span] for span in spans]

        finish_second(i, (0, 3), ys_at, sides_at[1, i])
        return carry

    def beside(x, left, right):
        from_east = jnp.where(lane_w == COLS - 1, right, pltpu.roll(x, COLS - 1, 1))
        from_west = jnp.where(lane_w == 0, left, pltpu.roll(x, 1, 1))
        return from_east, from_west

    def beyond(x, nxt, prev):
        upper = jnp.where(row_w == 7, jnp.broadcast_to(nxt, (SUB, COLS)), pltpu.roll(x, 7, 0))
        lower = jnp.where(row_w == 0, jnp.broadcast_to(prev, (SUB, COLS)), pltpu.roll(x, 1, 0))
        return upper, lower

    def ocean_sides(slot, i, l):
        right = jnp.broadcast_to(sides_at[slot, i, :, l:l + 1], (SUB, COLS))
        left = jnp.broadcast_to(sides_at[slot, i, :, 64 + l:65 + l], (SUB, COLS))
        return left, right

    def ocean_masks(i):
        wet = msk[i].astype(F32)
        m_e, m_w = beside(wet, *ocean_sides(0, i, LEV))
        nxt = jnp.where(
            i == TILES - 1, mirror[0, LEV:LEV + 1, :],
            msk[jnp.minimum(i + 1, TILES - 1), 0:1, :].astype(F32),
        )
        prev = jnp.where(i == 0, 0.0, msk[jnp.maximum(i - 1, 0), 7:8, :].astype(F32))
        m_n, m_s = beyond(wet, nxt, prev)
        return wet * m_e, wet * m_w, wet * m_n, wet * m_s

    def ocean_change(a, e, w, n, s, l, i, masks):
        d_e = masks[0] * (e - a)
        d_w = masks[1] * (w - a)
        d_n = masks[2] * (n - a)
        d_s = masks[3] * (s - a)
        return 0.15 * (d_e + d_w + d_n + d_s) - 0.25 * (
            vel[0, l, i] * (d_e - d_w) + vel[1, l, i] * (d_n - d_s)
        )

    def ocean_first(i, carry):
        masks = ocean_masks(i)
        for l in range(LEV):
            a = u[l, i]
            nxt = jnp.where(
                i == TILES - 1, mirror[0, l:l + 1, :], u[l, jnp.minimum(i + 1, TILES - 1), 0:1, :]
            )
            prev = jnp.where(i == 0, a[0:1], u[l, jnp.maximum(i - 1, 0), 7:8, :])
            e, w = beside(a, *ocean_sides(0, i, l))
            n, s = beyond(a, nxt, prev)
            change = ocean_change(a, e, w, n, s, l, i, masks)
            work[l, i] = change
            st[l, i + 1] = a + change
        return carry

    def ocean_second(i, carry):
        masks = ocean_masks(i)
        partial = [[] for _ in range(GROUPS)]
        carried = [None] * GROUPS
        for l in range(LEV):
            a = st[l, i + 1]
            e, w = beside(a, *ocean_sides(1, i, l))
            n, s = beyond(a, st[l, i + 2, 0:1, :], st[l, i, 7:8, :])
            change = ocean_change(a, e, w, n, s, l, i, masks)
            value = u[l, i] + 0.5 * (work[l, i] + change)
            if l == 0:
                value = value + delta[i + 1]
            for j in range(GROUPS):
                carried[j] = eliminate(i, l, j, value[:, spans[j]], carried[j])
                partial[j].append(carried[j])
        for j in range(GROUPS):
            back_substitute(i, j, partial[j])
        return carry

    for load in loads[2:9]:
        load.wait()
    high = deriv[...].astype(BF16)
    dmat[0:LANES, 0:LANES] = high
    dmat[0:LANES, LANES:2 * LANES] = (deriv[...] - high.astype(F32)).astype(BF16)
    dmat[LANES:2 * LANES, 0:LANES] = high
    dmat[LANES:2 * LANES, LANES:2 * LANES] = jnp.zeros((LANES, LANES), BF16)

    start_0, wait_0, drain_0 = halo_exchange(0)
    start_1, wait_1, drain_1 = halo_exchange(1)
    start_d, wait_d, drain_d = delta_exchange()

    @pl.when(is_ocean)
    def _():
        pack_edges(u, 0, 0, 1)
        start_0()

    def first_tendency(p, carry):
        tendency([(2 * p + r, j) for r in range(2) for j in range(GROUPS)], False)
        return carry

    @pl.when(is_atmos)
    def _():
        lax.fori_loop(0, TILES // 2, first_tendency, 0)
        pack_edges(st, 1, 0, 0)
        start_0()

    center.wait_recv()
    for copy in forwards:
        copy.start()

    lax.fori_loop(0, TILES, factors, 0, unroll=2)

    ident = ids[...]
    relative = (lax.shift_right_logical(ident, 8) - tile + 1 + N_TILE) & (N_TILE - 1)
    block = ident & (BLOCKS - 1)
    pos_v[...] = (
        jnp.minimum(relative, 2) * BLOCKS + (block & 3) * 64 + lax.shift_right_logical(block, 2)
    )
    pos_copy = local(pos_v, pos, lsem.at[9])
    pos_copy.start()

    pos_copy.wait()

    def widen(slot):
        for f in range(2):
            win[f, slot * BLOCKS:(slot + 1) * BLOCKS, :] = (
                winb[slot, f].reshape(BLOCKS, LANES).astype(F32)
            )

    widen(1)

    @pl.when(is_ocean)
    def _():
        wait_0()
        spread_sides(0, False)
        lax.fori_loop(0, TILES, ocean_first, 0)
        pack_edges(st, 1, 1, 0)
        start_1()

    for copy in forwards:
        copy.wait_recv()
    widen(0)
    widen(2)

    def regrid_rows(j, b, rows_in):
        for s in rows_in:
            block = (b * 8 + s) * GROUPS + j
            sides = []
            for k in range(2):
                p = pos[k, block]
                rows = [win[0, pl.ds(p, 1), :], win[1, pl.ds(p, 1), :]]
                sides.append(jnp.concatenate(rows + rows[:1] * 6, axis=0))
            picked = jnp.concatenate(sides, axis=1).astype(BF16)
            tiles = jnp.concatenate([wbuf[j, b, s, 0], wbuf[j, b, s, 1]], axis=1)
            result = lax.dot_general(
                picked, tiles, (((1,), (1,)), ((), ())), preferred_element_type=F32
            )
            cpl[0, b, s:s + 1, spans[j]] = result[0:1]
            cpl[1, b, s:s + 1, spans[j]] = result[1:2]

    def regrid(j):
        def body(b, carry):
            regrid_rows(j, b, range(8))
            return carry

        lax.fori_loop(0, TILES, body, 0, unroll=4)

    for j in order:
        wloads[j].wait()
    regrid(0)
    regrid(3)
    for j in (1, 2):
        regrid_rows(j, TILES - 1, (7,))

    packed = jnp.zeros((SUB, LANES), F32)
    for i in range(TILES):
        packed = jnp.where(
            (lane & 63) == i, side_pack(delta_at(i, spans[0]), delta_at(i, spans[-1])), packed
        )
    delta_out[0] = packed
    rows = [delta_at(TILES - 1, spans[j])[7:8] for j in range(GROUPS - 1, -1, -1)]
    delta_out[1] = lanes_of(jnp.concatenate(rows + rows, axis=0), flip)
    delta_out[2, 0:1, :] = pltpu.roll(packed, 64, 1)[SUB - 1:SUB]
    start_d()
    regrid(1)
    regrid(2)

    def all_delta(i, carry):
        for span in spans:
            delta[i + 1, :, span] = delta_at(i, span)
        return carry

    lax.fori_loop(0, TILES, all_delta, 0)

    @pl.when(is_atmos)
    def _():
        wait_0()
        spread_sides(0, True)
        fill_south()
        fill_north(0)
        lax.fori_loop(0, TILES, forward_first, 0, unroll=4)

    wait_d()
    sides = jnp.where(low_half, delta_in[0], delta_in[1])
    for j in range(GROUPS):
        delta[TILES + 1, 0:1, spans[j]] = delta_in[2, j:j + 1, :]
    delta[0, 7:8, :] = delta[1, 0:1, :]

    @pl.when(is_atmos)
    def _():
        corner = jnp.where(low_half, delta_in[3], delta_in[4])
        following = jnp.where((lane & 63) == TILES - 1, corner, pltpu.roll(sides, LANES - 1, 1))
        previous = jnp.where(
            (lane & 63) == 0, jnp.broadcast_to(sides[0:1], (SUB, LANES)), pltpu.roll(sides, 1, 1)
        )
        summed = row_pair_sum(sides, following, previous)
        for i in range(TILES):
            delta_side[i] = side_pick(summed, i)

        last = TILES - 1

        def finish_sides(i, carry):
            finish_first(i, (0, 3))
            return carry

        def finish_inner(i, carry):
            finish_first(i, (1, 2))
            return carry

        def tend_sides(p, carry):
            tendency([(4 * p + r, j) for r in range(4) for j in (0, 3)], True)
            return carry

        def tend_inner(p, carry):
            tendency([(4 * p + r, j) for r in range(4) for j in (1, 2)], True)
            return carry

        lax.fori_loop(0, TILES, finish_sides, 0, unroll=4)
        finish_first(last, (1, 2))
        tendency([(last, 1), (last, 2)], True)
        lax.fori_loop(0, TILES // 4, tend_sides, 0)
        pack_edges(st, 1, 1, 0)
        start_1()
        lax.fori_loop(0, last, finish_inner, 0, unroll=7)
        lax.fori_loop(0, TILES // 4, tend_inner, 0)
        fill_south()
        lax.fori_loop(0, last, second_middle, 0, unroll=7)
        wait_1()
        spread_sides(1, True)
        fill_north(1)
        for l in range(LEV):
            ys = row_sums(l, last)
            for j in range(GROUPS):
                work[l, last, :, spans[j]] = ys[j]
        lax.fori_loop(0, TILES, second_sides, 0, unroll=4)
        finish_second(last, (1, 2), lambda l: [work[l, last, :, span] for span in spans], None)

    @pl.when(is_ocean)
    def _():
        wait_1()

        def add_forcing(i, carry):
            st[0, i + 1] = st[0, i + 1] + delta[i + 1]
            return carry

        lax.fori_loop(0, TILES, add_forcing, 0)
        mirror[1, 0:1, :] = mirror[1, 0:1, :] + delta[TILES + 1, 0:1, :]
        fill_south()
        fill_north(1)
        spread_sides(1, False)
        for i in range(TILES):
            sides_at[1, i] = sides_at[1, i] + jnp.where(
                (lane & 63) == 0, side_pick(sides, i), 0.0
            )
        lax.fori_loop(0, TILES, ocean_second, 0)

    center.wait_send()
    for copy in forwards:
        copy.wait_send()
    drain_0()
    drain_d()
    drain_1()


def on_device(fields, velocity, mixing, surface_mask, intersection_ids, intersection_weights):
    vmem = pl.BlockSpec(memory_space=pltpu.VMEM)
    hbm = pl.BlockSpec(memory_space=pltpu.HBM)
    scratch = [
        pltpu.VMEM((2, LEV, TILES, SUB, COLS), F32),
        pltpu.VMEM((LEV - 1, TILES, SUB, COLS), F32),
        pltpu.VMEM((LEV - 1, TILES, SUB, COLS), F32),
        pltpu.VMEM((TILES, SUB, COLS), jnp.int32),
        pltpu.VMEM((GROUPS, TILES, SUB, 2, LANES, LANES), BF16),
        pltpu.VMEM((2, TILES, SUB, COLS), F32),
        pltpu.VMEM((2, GROUPS, 64, LANES), BF16),
        pltpu.VMEM((3, 2, GROUPS, 64, LANES), BF16),
        pltpu.VMEM((2, 3 * BLOCKS, LANES), F32),
        pltpu.VMEM((LEV, TILES + 2, SUB, COLS), F32),
        pltpu.VMEM((LEV, TILES, SUB, COLS), F32),
        pltpu.VMEM((LEV, TILES, SUB, COLS), F32),
        pltpu.VMEM((2, BLOCKS), jnp.int32),
        pltpu.VMEM((2, BLOCKS), jnp.int32),
        pltpu.SMEM((2, BLOCKS), jnp.int32),
        pltpu.VMEM((4, SUB, LANES), F32),
        pltpu.VMEM((LANES, LANES), F32),
        pltpu.VMEM((2 * LANES, 2 * LANES), BF16),
        pltpu.VMEM((TILES, SUB, LANES), F32),
        pltpu.VMEM((2, 2, SUB, LANES), F32),
        pltpu.VMEM((2, 16, COLS), F32),
        pltpu.VMEM((2, 4, SUB, LANES), F32),
        pltpu.VMEM((2, TILES, SUB, LANES), F32),
        pltpu.VMEM((2, 16, COLS), F32),
        pltpu.VMEM((TILES + 2, SUB, COLS), F32),
        pltpu.VMEM((3, SUB, LANES), F32),
        pltpu.VMEM((5, SUB, LANES), F32),
        pltpu.VMEM((TILES, SUB, LANES), F32),
        pltpu.SemaphoreType.DMA((10,)),
        pltpu.SemaphoreType.DMA((GROUPS,)),
        pltpu.SemaphoreType.DMA((3,)),
        pltpu.SemaphoreType.DMA((3,)),
        pltpu.SemaphoreType.DMA((15,)),
        pltpu.SemaphoreType.DMA((15,)),
    ]
    advanced, coupled = pl.pallas_call(
        kernel,
        out_shape=(
            pltpu.VMEM((LEV, TILES, SUB, COLS), F32),
            pltpu.VMEM((2, TILES, SUB, COLS), F32),
        ),
        in_specs=[hbm] * 8,
        out_specs=(vmem, vmem),
        scratch_shapes=scratch,
        compiler_params=pltpu.CompilerParams(
            collective_id=0, has_side_effects=True, vmem_limit_bytes=52 << 20
        ),
    )(
        jnp.transpose(intersection_ids[0], (1, 0)),
        jnp.asarray(across_table()),
        jnp.asarray(along_matrix()),
        fields.reshape(LEV, TILES, SUB, COLS),
        velocity.reshape(2, LEV, TILES, SUB, COLS),
        mixing.reshape(LEV - 1, TILES, SUB, COLS),
        surface_mask.reshape(TILES, SUB, COLS),
        intersection_weights.reshape(TILES, SUB, GROUPS, 2, LANES, LANES),
    )
    return (
        advanced.reshape(1, LEV, TILES * SUB, COLS),
        coupled.reshape(1, 2, TILES * SUB, COLS),
    )


def solution(mesh):
    placed = (
        P("comp", None, None, "tile"),
        P("comp", None, None, None, "tile"),
        P("comp", None, None, "tile"),
        P("comp", None, "tile"),
        P("comp", "tile", None),
        P("comp", "tile", None, None, None),
    )
    return jax.shard_map(
        on_device,
        mesh=mesh,
        in_specs=placed,
        out_specs=(P("comp", None, None, "tile"), P("comp", None, None, "tile")),
        check_vma=False,
    )
```

```python
import functools
import math

import jax
import jax.numpy as jnp
import numpy as np
from jax import lax
from jax.experimental import pallas as pl
from jax.experimental.pallas import tpu as pltpu
from jax.sharding import PartitionSpec as P

LEV = 14
TILES = 8
SUB = 8
COLS = 512
LANES = 128
GROUPS = 4
BLOCKS = 256
N_TILE = 64
MESH = pl.DeviceIdType.MESH
F32 = jnp.float32
BF16 = jnp.bfloat16


def gll_table():
    nodes = [-1.0, -1.0 / math.sqrt(5.0), 1.0 / math.sqrt(5.0), 1.0]
    weights = [math.prod(nodes[i] - nodes[j] for j in range(4) if j != i) for i in range(4)]
    table = np.zeros((4, 4))
    for i in range(4):
        for j in range(4):
            if i == j:
                table[i, j] = sum(1.0 / (nodes[i] - nodes[k]) for k in range(4) if k != i)
            else:
                table[i, j] = weights[i] / weights[j] / (nodes[i] - nodes[j])
    return table


def along_matrix():
    full = np.kron(np.eye(LANES // 4), gll_table().T).astype(np.float32)
    return full


def across_table():
    table = gll_table()
    coefs = np.zeros((4, SUB, LANES), np.float32)
    for row in range(SUB):
        for m in range(4):
            coefs[m, row, :] = table[row % 4, m]
    return coefs


def kernel(
    ids_in, coef_in, deriv_in, fields, velocity, mixing, mask_in, weights,
    u, cpl,
    vel, kap, elim, msk, wbuf, surf, src, winb, win, st, work, inv,
    ids, pos_v, pos, coef, deriv, dmat, pack, dense, top, halo, sides_at, mirror,
    delta, delta_out, delta_in, delta_side,
    lsem, wsem, e0s, e0r, xs, xr,
):
    comp = lax.axis_index("comp")
    tile = lax.axis_index("tile")
    other = 1 - comp
    east = lax.rem(tile + 1, N_TILE)
    west = lax.rem(tile + N_TILE - 1, N_TILE)
    fold = N_TILE - 1 - tile
    fold_lo = lax.rem(fold + N_TILE - 1, N_TILE)
    fold_hi = lax.rem(fold + 1, N_TILE)
    is_atmos = comp == 0
    is_ocean = comp == 1
    level_s = jnp.where(is_atmos, LEV - 1, 0)
    spans = [slice(j * LANES, (j + 1) * LANES) for j in range(GROUPS)]

    def local(src_ref, dst_ref, sem):
        return pltpu.make_async_copy(src_ref, dst_ref, sem)

    def remote(src_ref, dst_ref, send, recv, target):
        return pltpu.make_async_remote_copy(
            src_ref=src_ref, dst_ref=dst_ref, send_sem=send, recv_sem=recv,
            device_id=target, device_id_type=MESH,
        )

    loads = [
        local(fields.at[level_s], surf.at[0], lsem.at[0]),
        local(velocity.at[0, level_s], surf.at[1], lsem.at[1]),
        local(fields, u, lsem.at[2]),
        local(mask_in, msk, lsem.at[3]),
        local(mixing, kap, lsem.at[4]),
        local(velocity, vel, lsem.at[5]),
        local(ids_in, ids, lsem.at[6]),
        local(coef_in, coef, lsem.at[7]),
        local(deriv_in, deriv, lsem.at[8]),
    ]
    order = (0, 3, 1, 2)
    wloads = [local(weights.at[:, :, j], wbuf.at[j], wsem.at[j]) for j in range(GROUPS)]
    for load in loads:
        load.start()

    for j in order:
        wloads[j].start()

    barrier = pltpu.get_barrier_semaphore()
    for target in (
        (other, tile), (comp, east), (comp, west), (comp, fold),
    ):
        pl.semaphore_signal(barrier, inc=1, device_id=target, device_id_type=MESH)

    @pl.when(fold_lo != tile)
    def _():
        pl.semaphore_signal(barrier, inc=1, device_id=(comp, fold_lo), device_id_type=MESH)

    @pl.when(fold_hi != tile)
    def _():
        pl.semaphore_signal(barrier, inc=1, device_id=(comp, fold_hi), device_id_type=MESH)

    loads[0].wait()
    loads[1].wait()
    for f in range(2):
        for j in range(GROUPS):
            src[f, j] = surf[f, :, :, spans[j]].reshape(64, LANES).astype(BF16)

    selfs = jnp.where(fold_lo == tile, 1, 0) + jnp.where(fold_hi == tile, 1, 0)
    pl.semaphore_wait(barrier, 6 - selfs)

    center = remote(src, winb.at[1], e0s.at[1], e0r.at[1], (other, tile))
    center.start()
    forwards = [
        remote(winb.at[1], winb.at[0], e0s.at[0], e0r.at[0], (comp, east)),
        remote(winb.at[1], winb.at[2], e0s.at[2], e0r.at[2], (comp, west)),
    ]

    lane = lax.broadcasted_iota(jnp.int32, (SUB, LANES), 1)
    row = lax.broadcasted_iota(jnp.int32, (SUB, LANES), 0)
    lane_w = lax.broadcasted_iota(jnp.int32, (SUB, COLS), 1)
    row_w = lax.broadcasted_iota(jnp.int32, (SUB, COLS), 0)
    flip = (LANES - 1) - lane
    low_half = lane < 64
    pair_lane = jnp.where(
        (lane & 3) == 3, (lane + 1) & (LANES - 1),
        jnp.where((lane & 3) == 0, (lane + LANES - 1) & (LANES - 1), lane),
    )
    pair_row = jnp.where(
        (row & 3) == 3, (row + 1) & 7, jnp.where((row & 3) == 0, (row + 7) & 7, row)
    )
    ends = jnp.where(low_half, 0, LANES - 1)
    element = row & 4

    def lanes_of(x, index):
        return jnp.take_along_axis(x, index, axis=1)

    def rows_of(x, index):
        return jnp.take_along_axis(x, index, axis=0)

    def row_pair_sum(x, following, previous):
        mixed = jnp.where(row == 0, following, jnp.where(row == SUB - 1, previous, x))
        return x + rows_of(mixed, pair_row)

    def column_pair_sum(ys, sides, groups=range(GROUPS)):
        result = {}
        for j in groups:
            after = ys[j + 1] if j < GROUPS - 1 else sides
            before = ys[j - 1] if j > 0 else sides
            mixed = jnp.where(lane == 0, after, jnp.where(lane == LANES - 1, before, ys[j]))
            result[j] = ys[j] + lanes_of(mixed, pair_lane)
        return result

    def factors(i, carry):
        above = None
        ratio = None
        for l in range(LEV):
            diagonal = 1.0
            if l < LEV - 1:
                below = kap[l, i]
                diagonal = below + 1.0
            if l > 0:
                diagonal = diagonal + above * (1.0 - ratio)
            inverse = 1.0 / diagonal
            inv[l, i] = inverse
            if l > 0:
                elim[l - 1, i] = above * inverse
            if l < LEV - 1:
                ratio = below * inverse
                above = below
                kap[l, i] = ratio
        return carry

    def tendency(units, heated):
        xs = [u[:, i, :, spans[j]] for i, j in units]
        flat = jnp.concatenate([x.reshape(LEV * SUB, LANES) for x in xs], axis=0)
        high = flat.astype(BF16)
        low = (flat - high.astype(F32)).astype(BF16)
        product = jnp.dot(
            jnp.concatenate([high, low], axis=1), dmat[...], preferred_element_type=F32
        )
        for n, (i, j) in enumerate(units):
            span = spans[j]
            part = product[n * LEV * SUB:(n + 1) * LEV * SUB]
            along = (part[:, :LANES] + part[:, LANES:]).reshape(LEV, SUB, LANES)
            for l in range(LEV):
                xl = xs[n][l]
                across = rows_of(xl, element) * coef[0]
                for m in range(1, 4):
                    across += rows_of(xl, element + m) * coef[m]
                value = xl - 0.08 * (
                    vel[0, l, i, :, span] * along[l] + vel[1, l, i, :, span] * across
                )
                if heated and l == LEV - 1:
                    value = value + heat_rate(i, span) * (cpl[0, i, :, span] - xl)
                st[l, i + 1, :, span] = value

    def rate_of(i, span, wind):
        wet = msk[i, :, span].astype(F32)
        return 0.5 * (1.0 + jnp.abs(surf[1, i, :, span] - wind)) * wet

    def heat_rate(i, span):
        return rate_of(i, span, cpl[1, i, :, span])

    def delta_at(i, span):
        return heat_rate(i, span) * (cpl[0, i, :, span] - surf[0, i, :, span])

    def turned(x, amount):
        amount = amount % LANES
        return x if amount == 0 else pltpu.roll(x, amount, 1)

    def side_pack(left, right):
        return lanes_of(jnp.where(lane == 0, left, right), ends)

    def pack_edges(values, shift, slot, with_mask):
        def body(i, carry):
            packed = jnp.zeros((SUB, LANES), F32)
            for l in range(LEV + with_mask):
                if l < LEV:
                    left = values[l, i + shift, :, spans[0]]
                    right = values[l, i + shift, :, spans[-1]]
                else:
                    left = msk[i, :, spans[0]].astype(F32)
                    right = msk[i, :, spans[-1]].astype(F32)
                packed = jnp.where((lane & 63) == l, side_pack(left, right), packed)
            pack[i] = packed
            return carry

        lax.fori_loop(0, TILES, body, 0, unroll=8)
        dense_w = jnp.zeros((SUB, LANES), F32)
        dense_e = jnp.zeros((SUB, LANES), F32)
        for i in range(TILES):
            here = lax.shift_right_logical(lane, 4) == i
            dense_w = jnp.where(here, turned(pack[i], 16 * i), dense_w)
            dense_e = jnp.where(here, turned(pack[i], 16 * i - 64), dense_e)
        dense[slot, 0] = dense_w
        dense[slot, 1] = dense_e
        for half in range(2):
            for j in range(GROUPS):
                rows = []
                for s in range(8):
                    l = half * 8 + s
                    if l < LEV:
                        rows.append(values[l, TILES - 1 + shift, 7:8, spans[j]])
                    elif l == LEV:
                        rows.append(msk[TILES - 1, 7:8, spans[j]].astype(F32))
                    else:
                        rows.append(jnp.zeros((1, LANES), F32))
                block = jnp.concatenate(rows, axis=0)
                top[slot, half * 8:half * 8 + 8, spans[GROUPS - 1 - j]] = lanes_of(block, flip)

    def exchange(base, to_west, to_east, to_fold, to_lo, to_hi, at):
        copies = [
            remote(to_fold, at[2], xs.at[base + 2], xr.at[base + 2], (comp, fold)),
            remote(to_west, at[0], xs.at[base], xr.at[base], (comp, west)),
            remote(to_east, at[1], xs.at[base + 1], xr.at[base + 1], (comp, east)),
        ]
        lo = remote(to_lo, at[3], xs.at[base + 3], xr.at[base + 3], (comp, fold_lo))
        hi = remote(to_hi, at[4], xs.at[base + 4], xr.at[base + 4], (comp, fold_hi))

        def start():
            for copy in copies:
                copy.start()

            @pl.when(fold_lo != tile)
            def _():
                lo.start()

            @pl.when(fold_hi != tile)
            def _():
                hi.start()

            @pl.when(fold_lo == tile)
            def _():
                at[3][...] = to_lo[...]

            @pl.when(fold_hi == tile)
            def _():
                at[4][...] = to_hi[...]

        def wait():
            for copy in copies:
                copy.wait_recv()

            @pl.when(fold_lo != tile)
            def _():
                lo.wait_recv()

            @pl.when(fold_hi != tile)
            def _():
                hi.wait_recv()

        def drain():
            for copy in copies:
                copy.wait_send()

            @pl.when(fold_lo != tile)
            def _():
                lo.wait_send()

            @pl.when(fold_hi != tile)
            def _():
                hi.wait_send()

        return start, wait, drain

    def halo_exchange(slot):
        return exchange(
            slot * 5, dense.at[slot, 0], dense.at[slot, 1], top.at[slot],
            dense.at[slot, 1], dense.at[slot, 0],
            [halo.at[slot, 0], halo.at[slot, 1], mirror.at[slot], halo.at[slot, 2], halo.at[slot, 3]],
        )

    def delta_exchange():
        return exchange(
            10, delta_out.at[0], delta_out.at[0], delta_out.at[1], delta_out.at[2], delta_out.at[2],
            [delta_in.at[n] for n in range(5)],
        )

    def fill_south():
        for l in range(LEV):
            st[l, 0, 7:8, :] = st[l, 1, 0:1, :]

    def fill_north(slot):
        for l in range(LEV):
            st[l, TILES + 1, 0:1, :] = mirror[slot, l:l + 1, :]

    def spread_sides(slot, summed):
        both = []
        for n in range(2):
            h = halo[slot, n]
            if summed:
                corner = pltpu.roll(halo[slot, 2 + n], 1, 0)
                following = jnp.where(lane >= LANES - 16, corner, turned(h, -16))
                previous = jnp.where(
                    lane < 16, jnp.broadcast_to(h[0:1], (SUB, LANES)), turned(h, 16)
                )
                h = row_pair_sum(h, following, previous)
            both.append(h)
        for i in range(TILES):
            sides_at[slot, i] = jnp.where(
                low_half, turned(both[0], -16 * i), turned(both[1], 64 - 16 * i)
            )

    def side_pick(halos, l):
        return lanes_of(halos, jnp.where(low_half, l, 64 + l))

    def row_sums(l, i):
        return [
            row_pair_sum(st[l, i + 1, :, span], st[l, i + 2, :, span], st[l, i, :, span])
            for span in spans
        ]

    def eliminate(i, l, j, value, carried):
        value = value * inv[l, i, :, spans[j]]
        if l > 0:
            value = value + elim[l - 1, i, :, spans[j]] * carried
        return value

    def back_substitute(i, j, partial):
        span = spans[j]
        result = partial[LEV - 1]
        u[LEV - 1, i, :, span] = result
        for l in range(LEV - 2, -1, -1):
            result = partial[l] + kap[l, i, :, span] * result
            u[l, i, :, span] = result

    def forward_first(i, carry):
        halos = sides_at[0, i]
        carried = [None] * GROUPS
        for l in range(LEV):
            sums = column_pair_sum(row_sums(l, i), side_pick(halos, l))
            for j in range(GROUPS):
                carried[j] = 0.25 * sums[j]
                if l < LEV - 1:
                    carried[j] = eliminate(i, l, j, carried[j], previous[j] if l else None)
                work[l, i, :, spans[j]] = carried[j]
            previous = list(carried)
        return carry

    def finish_first(i, groups):
        ys = [
            row_pair_sum(delta[i + 1, :, span], delta[i + 2, :, span], delta[i, :, span])
            for span in spans
        ]
        sums = column_pair_sum(ys, delta_side[i], groups)
        for j in groups:
            span = spans[j]
            partial = [work[l, i, :, span] for l in range(LEV - 1)]
            value = work[LEV - 1, i, :, span] + 0.25 * sums[j]
            partial.append(eliminate(i, LEV - 1, j, value, partial[-1]))
            back_substitute(i, j, partial)

    def finish_second(i, groups, ys_at, halos):
        carried = {j: None for j in groups}
        partial = {j: [] for j in groups}
        for l in range(LEV):
            sides = halos if halos is None else side_pick(halos, l)
            sums = column_pair_sum(ys_at(l), sides, groups)
            for j in groups:
                carried[j] = eliminate(i, l, j, 0.25 * sums[j], carried[j])
                partial[j].append(carried[j])
        for j in groups:
            back_substitute(i, j, partial[j])

    def second_middle(i, carry):
        def ys_at(l):
            ys = row_sums(l, i)
            for j in range(GROUPS):
                work[l, i, :, spans[j]] = ys[j]
            return ys

        finish_second(i, (1, 2), ys_at, None)
        return carry

    def second_sides(i, carry):
        def ys_at(l):
            return [work[l, i, :, span] for span in spans]

        finish_second(i, (0, 3), ys_at, sides_at[1, i])
        return carry

    def beside(x, left, right):
        from_east = jnp.where(lane_w == COLS - 1, right, pltpu.roll(x, COLS - 1, 1))
        from_west = jnp.where(lane_w == 0, left, pltpu.roll(x, 1, 1))
        return from_east, from_west

    def beyond(x, nxt, prev):
        upper = jnp.where(row_w == 7, jnp.broadcast_to(nxt, (SUB, COLS)), pltpu.roll(x, 7, 0))
        lower = jnp.where(row_w == 0, jnp.broadcast_to(prev, (SUB, COLS)), pltpu.roll(x, 1, 0))
        return upper, lower

    def ocean_sides(slot, i, l):
        right = jnp.broadcast_to(sides_at[slot, i, :, l:l + 1], (SUB, COLS))
        left = jnp.broadcast_to(sides_at[slot, i, :, 64 + l:65 + l], (SUB, COLS))
        return left, right

    def ocean_masks(i):
        wet = msk[i].astype(F32)
        m_e, m_w = beside(wet, *ocean_sides(0, i, LEV))
        nxt = jnp.where(
            i == TILES - 1, mirror[0, LEV:LEV + 1, :],
            msk[jnp.minimum(i + 1, TILES - 1), 0:1, :].astype(F32),
        )
        prev = jnp.where(i == 0, 0.0, msk[jnp.maximum(i - 1, 0), 7:8, :].astype(F32))
        m_n, m_s = beyond(wet, nxt, prev)
        return wet * m_e, wet * m_w, wet * m_n, wet * m_s

    def ocean_change(a, e, w, n, s, l, i, masks):
        d_e = masks[0] * (e - a)
        d_w = masks[1] * (w - a)
        d_n = masks[2] * (n - a)
        d_s = masks[3] * (s - a)
        return 0.15 * (d_e + d_w + d_n + d_s) - 0.25 * (
            vel[0, l, i] * (d_e - d_w) + vel[1, l, i] * (d_n - d_s)
        )

    def ocean_first(i, carry):
        masks = ocean_masks(i)
        for l in range(LEV):
            a = u[l, i]
            nxt = jnp.where(
                i == TILES - 1, mirror[0, l:l + 1, :], u[l, jnp.minimum(i + 1, TILES - 1), 0:1, :]
            )
            prev = jnp.where(i == 0, a[0:1], u[l, jnp.maximum(i - 1, 0), 7:8, :])
            e, w = beside(a, *ocean_sides(0, i, l))
            n, s = beyond(a, nxt, prev)
            change = ocean_change(a, e, w, n, s, l, i, masks)
            work[l, i] = change
            st[l, i + 1] = a + change
        return carry

    def ocean_second(i, carry):
        masks = ocean_masks(i)
        partial = [[] for _ in range(GROUPS)]
        carried = [None] * GROUPS
        for l in range(LEV):
            a = st[l, i + 1]
            e, w = beside(a, *ocean_sides(1, i, l))
            n, s = beyond(a, st[l, i + 2, 0:1, :], st[l, i, 7:8, :])
            change = ocean_change(a, e, w, n, s, l, i, masks)
            value = u[l, i] + 0.5 * (work[l, i] + change)
            if l == 0:
                value = value + delta[i + 1]
            for j in range(GROUPS):
                carried[j] = eliminate(i, l, j, value[:, spans[j]], carried[j])
                partial[j].append(carried[j])
        for j in range(GROUPS):
            back_substitute(i, j, partial[j])
        return carry

    for load in loads[2:9]:
        load.wait()
    high = deriv[...].astype(BF16)
    dmat[0:LANES, 0:LANES] = high
    dmat[0:LANES, LANES:2 * LANES] = (deriv[...] - high.astype(F32)).astype(BF16)
    dmat[LANES:2 * LANES, 0:LANES] = high
    dmat[LANES:2 * LANES, LANES:2 * LANES] = jnp.zeros((LANES, LANES), BF16)

    start_0, wait_0, drain_0 = halo_exchange(0)
    start_1, wait_1, drain_1 = halo_exchange(1)
    start_d, wait_d, drain_d = delta_exchange()

    @pl.when(is_ocean)
    def _():
        pack_edges(u, 0, 0, 1)
        start_0()

    def first_tendency(p, carry):
        tendency([(2 * p + r, j) for r in range(2) for j in range(GROUPS)], False)
        return carry

    @pl.when(is_atmos)
    def _():
        lax.fori_loop(0, TILES // 2, first_tendency, 0)
        pack_edges(st, 1, 0, 0)
        start_0()

    center.wait_recv()
    for copy in forwards:
        copy.start()

    lax.fori_loop(0, TILES, factors, 0, unroll=2)

    ident = ids[...]
    relative = (lax.shift_right_logical(ident, 8) - tile + 1 + N_TILE) & (N_TILE - 1)
    block = ident & (BLOCKS - 1)
    pos_v[...] = (
        jnp.minimum(relative, 2) * BLOCKS + (block & 3) * 64 + lax.shift_right_logical(block, 2)
    )
    pos_copy = local(pos_v, pos, lsem.at[9])
    pos_copy.start()

    pos_copy.wait()

    def widen(slot):
        for f in range(2):
            win[f, slot * BLOCKS:(slot + 1) * BLOCKS, :] = (
                winb[slot, f].reshape(BLOCKS, LANES).astype(F32)
            )

    widen(1)

    @pl.when(is_atmos)
    def _():
        wait_0()
        spread_sides(0, True)
        fill_south()
        fill_north(0)
        lax.fori_loop(0, TILES, forward_first, 0, unroll=4)

    @pl.when(is_ocean)
    def _():
        wait_0()
        spread_sides(0, False)
        lax.fori_loop(0, TILES, ocean_first, 0)
        pack_edges(st, 1, 1, 0)
        start_1()

    for copy in forwards:
        copy.wait_recv()
    widen(0)
    widen(2)

    def regrid_rows(j, b, rows_in):
        for s in rows_in:
            block = (b * 8 + s) * GROUPS + j
            sides = []
            for k in range(2):
                p = pos[k, block]
                rows = [win[0, pl.ds(p, 1), :], win[1, pl.ds(p, 1), :]]
                sides.append(jnp.concatenate(rows + rows[:1] * 6, axis=0))
            picked = jnp.concatenate(sides, axis=1).astype(BF16)
            tiles = jnp.concatenate([wbuf[j, b, s, 0], wbuf[j, b, s, 1]], axis=1)
            result = lax.dot_general(
                picked, tiles, (((1,), (1,)), ((), ())), preferred_element_type=F32
            )
            cpl[0, b, s:s + 1, spans[j]] = result[0:1]
            cpl[1, b, s:s + 1, spans[j]] = result[1:2]

    def regrid(j):
        def body(b, carry):
            regrid_rows(j, b, range(8))
            return carry

        lax.fori_loop(0, TILES, body, 0, unroll=8)

    for j in order:
        wloads[j].wait()

    def edge_delta(i, j, rows, pick):
        sums = [[], []]
        for s in range(SUB):
            block = (i * SUB + s) * GROUPS + j
            lines = [wbuf[j, i, s, k, rows, :].astype(F32)[pick:pick + 1] for k in range(2)]
            for f in range(2):
                sums[f].append(
                    lines[0] * win[f, pl.ds(pos[0, block], 1), :]
                    + lines[1] * win[f, pl.ds(pos[1, block], 1), :]
                )
        target, wind = [
            jnp.broadcast_to(
                jnp.sum(jnp.concatenate(part, axis=0), axis=1, keepdims=True), (SUB, LANES)
            )
            for part in sums
        ]
        return rate_of(i, spans[j], wind) * (target - surf[0, i, :, spans[j]])

    def edge_pack(i, packed):
        left = edge_delta(i, 0, slice(0, 16), 0)
        right = edge_delta(i, GROUPS - 1, slice(LANES - 16, LANES), 15)
        return jnp.where((lane & 63) == i, side_pack(left, right), packed)

    for j in range(GROUPS):
        regrid_rows(j, TILES - 1, (SUB - 1,))
    rows = [delta_at(TILES - 1, spans[j])[7:8] for j in range(GROUPS - 1, -1, -1)]
    delta_out[1] = lanes_of(jnp.concatenate(rows + rows, axis=0), flip)
    packed = lax.fori_loop(0, TILES, edge_pack, jnp.zeros((SUB, LANES), F32), unroll=4)
    delta_out[0] = packed
    delta_out[2, 0:1, :] = pltpu.roll(packed, 64, 1)[SUB - 1:SUB]
    start_d()
    for j in order:
        regrid(j)

    def all_delta(i, carry):
        for span in spans:
            delta[i + 1, :, span] = delta_at(i, span)
        return carry

    lax.fori_loop(0, TILES, all_delta, 0)

    wait_d()
    sides = jnp.where(low_half, delta_in[0], delta_in[1])
    for j in range(GROUPS):
        delta[TILES + 1, 0:1, spans[j]] = delta_in[2, j:j + 1, :]
    delta[0, 7:8, :] = delta[1, 0:1, :]

    @pl.when(is_atmos)
    def _():
        corner = jnp.where(low_half, delta_in[3], delta_in[4])
        following = jnp.where((lane & 63) == TILES - 1, corner, pltpu.roll(sides, LANES - 1, 1))
        previous = jnp.where(
            (lane & 63) == 0, jnp.broadcast_to(sides[0:1], (SUB, LANES)), pltpu.roll(sides, 1, 1)
        )
        summed = row_pair_sum(sides, following, previous)
        for i in range(TILES):
            delta_side[i] = side_pick(summed, i)

        last = TILES - 1

        def finish_sides(i, carry):
            finish_first(i, (0, 3))
            return carry

        def finish_inner(i, carry):
            finish_first(i, (1, 2))
            return carry

        def tend_sides(p, carry):
            tendency([(4 * p + r, j) for r in range(4) for j in (0, 3)], True)
            return carry

        def tend_inner(p, carry):
            tendency([(4 * p + r, j) for r in range(4) for j in (1, 2)], True)
            return carry

        lax.fori_loop(0, TILES, finish_sides, 0, unroll=4)
        finish_first(last, (1, 2))
        tendency([(last, 1), (last, 2)], True)
        lax.fori_loop(0, TILES // 4, tend_sides, 0)
        pack_edges(st, 1, 1, 0)
        start_1()
        lax.fori_loop(0, last, finish_inner, 0, unroll=7)
        lax.fori_loop(0, TILES // 4, tend_inner, 0)
        fill_south()
        lax.fori_loop(0, last, second_middle, 0, unroll=7)
        wait_1()
        spread_sides(1, True)
        fill_north(1)
        for l in range(LEV):
            ys = row_sums(l, last)
            for j in range(GROUPS):
                work[l, last, :, spans[j]] = ys[j]
        lax.fori_loop(0, TILES, second_sides, 0, unroll=4)
        finish_second(last, (1, 2), lambda l: [work[l, last, :, span] for span in spans], None)

    @pl.when(is_ocean)
    def _():
        wait_1()

        def add_forcing(i, carry):
            st[0, i + 1] = st[0, i + 1] + delta[i + 1]
            return carry

        lax.fori_loop(0, TILES, add_forcing, 0)
        mirror[1, 0:1, :] = mirror[1, 0:1, :] + delta[TILES + 1, 0:1, :]
        fill_south()
        fill_north(1)
        spread_sides(1, False)
        for i in range(TILES):
            sides_at[1, i] = sides_at[1, i] + jnp.where(
                (lane & 63) == 0, side_pick(sides, i), 0.0
            )
        lax.fori_loop(0, TILES, ocean_second, 0)

    center.wait_send()
    for copy in forwards:
        copy.wait_send()
    drain_0()
    drain_d()
    drain_1()


def on_device(fields, velocity, mixing, surface_mask, intersection_ids, intersection_weights):
    vmem = pl.BlockSpec(memory_space=pltpu.VMEM)
    hbm = pl.BlockSpec(memory_space=pltpu.HBM)
    scratch = [
        pltpu.VMEM((2, LEV, TILES, SUB, COLS), F32),
        pltpu.VMEM((LEV - 1, TILES, SUB, COLS), F32),
        pltpu.VMEM((LEV - 1, TILES, SUB, COLS), F32),
        pltpu.VMEM((TILES, SUB, COLS), jnp.int32),
        pltpu.VMEM((GROUPS, TILES, SUB, 2, LANES, LANES), BF16),
        pltpu.VMEM((2, TILES, SUB, COLS), F32),
        pltpu.VMEM((2, GROUPS, 64, LANES), BF16),
        pltpu.VMEM((3, 2, GROUPS, 64, LANES), BF16),
        pltpu.VMEM((2, 3 * BLOCKS, LANES), F32),
        pltpu.VMEM((LEV, TILES + 2, SUB, COLS), F32),
        pltpu.VMEM((LEV, TILES, SUB, COLS), F32),
        pltpu.VMEM((LEV, TILES, SUB, COLS), F32),
        pltpu.VMEM((2, BLOCKS), jnp.int32),
        pltpu.VMEM((2, BLOCKS), jnp.int32),
        pltpu.SMEM((2, BLOCKS), jnp.int32),
        pltpu.VMEM((4, SUB, LANES), F32),
        pltpu.VMEM((LANES, LANES), F32),
        pltpu.VMEM((2 * LANES, 2 * LANES), BF16),
        pltpu.VMEM((TILES, SUB, LANES), F32),
        pltpu.VMEM((2, 2, SUB, LANES), F32),
        pltpu.VMEM((2, 16, COLS), F32),
        pltpu.VMEM((2, 4, SUB, LANES), F32),
        pltpu.VMEM((2, TILES, SUB, LANES), F32),
        pltpu.VMEM((2, 16, COLS), F32),
        pltpu.VMEM((TILES + 2, SUB, COLS), F32),
        pltpu.VMEM((3, SUB, LANES), F32),
        pltpu.VMEM((5, SUB, LANES), F32),
        pltpu.VMEM((TILES, SUB, LANES), F32),
        pltpu.SemaphoreType.DMA((10,)),
        pltpu.SemaphoreType.DMA((GROUPS,)),
        pltpu.SemaphoreType.DMA((3,)),
        pltpu.SemaphoreType.DMA((3,)),
        pltpu.SemaphoreType.DMA((15,)),
        pltpu.SemaphoreType.DMA((15,)),
    ]
    advanced, coupled = pl.pallas_call(
        kernel,
        out_shape=(
            pltpu.VMEM((LEV, TILES, SUB, COLS), F32),
            pltpu.VMEM((2, TILES, SUB, COLS), F32),
        ),
        in_specs=[hbm] * 8,
        out_specs=(vmem, vmem),
        scratch_shapes=scratch,
        compiler_params=pltpu.CompilerParams(
            collective_id=0, has_side_effects=True, vmem_limit_bytes=52 << 20
        ),
    )(
        jnp.transpose(intersection_ids[0], (1, 0)),
        jnp.asarray(across_table()),
        jnp.asarray(along_matrix()),
        fields.reshape(LEV, TILES, SUB, COLS),
        velocity.reshape(2, LEV, TILES, SUB, COLS),
        mixing.reshape(LEV - 1, TILES, SUB, COLS),
        surface_mask.reshape(TILES, SUB, COLS),
        intersection_weights.reshape(TILES, SUB, GROUPS, 2, LANES, LANES),
    )
    return (
        advanced.reshape(1, LEV, TILES * SUB, COLS),
        coupled.reshape(1, 2, TILES * SUB, COLS),
    )


def solution(mesh):
    placed = (
        P("comp", None, None, "tile"),
        P("comp", None, None, None, "tile"),
        P("comp", None, None, "tile"),
        P("comp", None, "tile"),
        P("comp", "tile", None),
        P("comp", "tile", None, None, None),
    )
    return jax.shard_map(
        on_device,
        mesh=mesh,
        in_specs=placed,
        out_specs=(P("comp", None, None, "tile"), P("comp", None, None, "tile")),
        check_vma=False,
    )
```

```python
import functools
import math

import jax
import jax.numpy as jnp
import numpy as np
from jax import lax
from jax.experimental import pallas as pl
from jax.experimental.pallas import tpu as pltpu
from jax.sharding import PartitionSpec as P

LEV = 14
TILES = 8
SUB = 8
COLS = 512
LANES = 128
GROUPS = 4
BLOCKS = 256
N_TILE = 64
MESH = pl.DeviceIdType.MESH
F32 = jnp.float32
BF16 = jnp.bfloat16


def gll_table():
    nodes = [-1.0, -1.0 / math.sqrt(5.0), 1.0 / math.sqrt(5.0), 1.0]
    weights = [math.prod(nodes[i] - nodes[j] for j in range(4) if j != i) for i in range(4)]
    table = np.zeros((4, 4))
    for i in range(4):
        for j in range(4):
            if i == j:
                table[i, j] = sum(1.0 / (nodes[i] - nodes[k]) for k in range(4) if k != i)
            else:
                table[i, j] = weights[i] / weights[j] / (nodes[i] - nodes[j])
    return table


def along_matrix():
    full = np.kron(np.eye(LANES // 4), gll_table().T).astype(np.float32)
    return full


def across_table():
    table = gll_table()
    coefs = np.zeros((4, SUB, LANES), np.float32)
    for row in range(SUB):
        for m in range(4):
            coefs[m, row, :] = table[row % 4, m]
    return coefs


def kernel(
    ids_in, coef_in, deriv_in, fields, velocity, mixing, mask_in, weights,
    u, cpl,
    vel, kap, elim, msk, wbuf, surf, src, winb, win, st, work, inv,
    ids, pos_v, pos, coef, deriv, dmat, pack, dense, top, halo, sides_at, mirror,
    delta, delta_out, delta_in, delta_side,
    lsem, wsem, e0s, e0r, xs, xr,
):
    comp = lax.axis_index("comp")
    tile = lax.axis_index("tile")
    other = 1 - comp
    east = lax.rem(tile + 1, N_TILE)
    west = lax.rem(tile + N_TILE - 1, N_TILE)
    fold = N_TILE - 1 - tile
    fold_lo = lax.rem(fold + N_TILE - 1, N_TILE)
    fold_hi = lax.rem(fold + 1, N_TILE)
    is_atmos = comp == 0
    is_ocean = comp == 1
    level_s = jnp.where(is_atmos, LEV - 1, 0)
    spans = [slice(j * LANES, (j + 1) * LANES) for j in range(GROUPS)]

    def local(src_ref, dst_ref, sem):
        return pltpu.make_async_copy(src_ref, dst_ref, sem)

    def remote(src_ref, dst_ref, send, recv, target):
        return pltpu.make_async_remote_copy(
            src_ref=src_ref, dst_ref=dst_ref, send_sem=send, recv_sem=recv,
            device_id=target, device_id_type=MESH,
        )

    loads = [
        local(fields.at[level_s], surf.at[0], lsem.at[0]),
        local(velocity.at[0, level_s], surf.at[1], lsem.at[1]),
        local(fields, u, lsem.at[2]),
        local(mask_in, msk, lsem.at[3]),
        local(mixing, kap, lsem.at[4]),
        local(velocity, vel, lsem.at[5]),
        local(ids_in, ids, lsem.at[6]),
        local(coef_in, coef, lsem.at[7]),
        local(deriv_in, deriv, lsem.at[8]),
    ]
    order = (0, 3, 1, 2)
    wloads = [local(weights.at[:, :, j], wbuf.at[j], wsem.at[j]) for j in range(GROUPS)]
    for n in (0, 1, 2, 5, 8, 7, 3, 4, 6):
        loads[n].start()

    for j in order:
        wloads[j].start()

    barrier = pltpu.get_barrier_semaphore()
    for target in (
        (other, tile), (comp, east), (comp, west), (comp, fold),
    ):
        pl.semaphore_signal(barrier, inc=1, device_id=target, device_id_type=MESH)

    @pl.when(fold_lo != tile)
    def _():
        pl.semaphore_signal(barrier, inc=1, device_id=(comp, fold_lo), device_id_type=MESH)

    @pl.when(fold_hi != tile)
    def _():
        pl.semaphore_signal(barrier, inc=1, device_id=(comp, fold_hi), device_id_type=MESH)

    loads[0].wait()
    loads[1].wait()
    for f in range(2):
        for j in range(GROUPS):
            src[f, j] = surf[f, :, :, spans[j]].reshape(64, LANES).astype(BF16)

    selfs = jnp.where(fold_lo == tile, 1, 0) + jnp.where(fold_hi == tile, 1, 0)
    pl.semaphore_wait(barrier, 6 - selfs)

    center = remote(src, winb.at[1], e0s.at[1], e0r.at[1], (other, tile))
    center.start()
    forwards = [
        remote(winb.at[1], winb.at[0], e0s.at[0], e0r.at[0], (comp, east)),
        remote(winb.at[1], winb.at[2], e0s.at[2], e0r.at[2], (comp, west)),
    ]

    lane = lax.broadcasted_iota(jnp.int32, (SUB, LANES), 1)
    row = lax.broadcasted_iota(jnp.int32, (SUB, LANES), 0)
    lane_w = lax.broadcasted_iota(jnp.int32, (SUB, COLS), 1)
    row_w = lax.broadcasted_iota(jnp.int32, (SUB, COLS), 0)
    flip = (LANES - 1) - lane
    low_half = lane < 64
    pair_lane = jnp.where(
        (lane & 3) == 3, (lane + 1) & (LANES - 1),
        jnp.where((lane & 3) == 0, (lane + LANES - 1) & (LANES - 1), lane),
    )
    pair_row = jnp.where(
        (row & 3) == 3, (row + 1) & 7, jnp.where((row & 3) == 0, (row + 7) & 7, row)
    )
    ends = jnp.where(low_half, 0, LANES - 1)
    element = row & 4

    def lanes_of(x, index):
        return jnp.take_along_axis(x, index, axis=1)

    def rows_of(x, index):
        return jnp.take_along_axis(x, index, axis=0)

    def row_pair_sum(x, following, previous):
        mixed = jnp.where(row == 0, following, jnp.where(row == SUB - 1, previous, x))
        return x + rows_of(mixed, pair_row)

    def column_pair_sum(ys, sides, groups=range(GROUPS)):
        result = {}
        for j in groups:
            after = ys[j + 1] if j < GROUPS - 1 else sides
            before = ys[j - 1] if j > 0 else sides
            mixed = jnp.where(lane == 0, after, jnp.where(lane == LANES - 1, before, ys[j]))
            result[j] = ys[j] + lanes_of(mixed, pair_lane)
        return result

    def factors(i, carry):
        above = None
        ratio = None
        for l in range(LEV):
            diagonal = 1.0
            if l < LEV - 1:
                below = kap[l, i]
                diagonal = below + 1.0
            if l > 0:
                diagonal = diagonal + above * (1.0 - ratio)
            inverse = 1.0 / diagonal
            inv[l, i] = inverse
            if l > 0:
                elim[l - 1, i] = above * inverse
            if l < LEV - 1:
                ratio = below * inverse
                above = below
                kap[l, i] = ratio
        return carry

    def tendency(units, heated):
        xs = [u[:, i, :, spans[j]] for i, j in units]
        flat = jnp.concatenate([x.reshape(LEV * SUB, LANES) for x in xs], axis=0)
        high = flat.astype(BF16)
        low = (flat - high.astype(F32)).astype(BF16)
        product = jnp.dot(
            jnp.concatenate([high, low], axis=1), dmat[...], preferred_element_type=F32
        )
        for n, (i, j) in enumerate(units):
            span = spans[j]
            part = product[n * LEV * SUB:(n + 1) * LEV * SUB]
            along = (part[:, :LANES] + part[:, LANES:]).reshape(LEV, SUB, LANES)
            for l in range(LEV):
                xl = xs[n][l]
                across = rows_of(xl, element) * coef[0]
                for m in range(1, 4):
                    across += rows_of(xl, element + m) * coef[m]
                value = xl - 0.08 * (
                    vel[0, l, i, :, span] * along[l] + vel[1, l, i, :, span] * across
                )
                if heated and l == LEV - 1:
                    value = value + heat_rate(i, span) * (cpl[0, i, :, span] - xl)
                st[l, i + 1, :, span] = value

    def rate_of(i, span, wind):
        wet = msk[i, :, span].astype(F32)
        return 0.5 * (1.0 + jnp.abs(surf[1, i, :, span] - wind)) * wet

    def heat_rate(i, span):
        return rate_of(i, span, cpl[1, i, :, span])

    def delta_at(i, span):
        return heat_rate(i, span) * (cpl[0, i, :, span] - surf[0, i, :, span])

    def turned(x, amount):
        amount = amount % LANES
        return x if amount == 0 else pltpu.roll(x, amount, 1)

    def side_pack(left, right):
        return lanes_of(jnp.where(lane == 0, left, right), ends)

    def pack_edges(values, shift, slot, with_mask):
        def body(i, carry):
            packed = jnp.zeros((SUB, LANES), F32)
            for l in range(LEV + with_mask):
                if l < LEV:
                    left = values[l, i + shift, :, spans[0]]
                    right = values[l, i + shift, :, spans[-1]]
                else:
                    left = msk[i, :, spans[0]].astype(F32)
                    right = msk[i, :, spans[-1]].astype(F32)
                packed = jnp.where((lane & 63) == l, side_pack(left, right), packed)
            pack[i] = packed
            return carry

        lax.fori_loop(0, TILES, body, 0, unroll=8)
        dense_w = jnp.zeros((SUB, LANES), F32)
        dense_e = jnp.zeros((SUB, LANES), F32)
        for i in range(TILES):
            here = lax.shift_right_logical(lane, 4) == i
            dense_w = jnp.where(here, turned(pack[i], 16 * i), dense_w)
            dense_e = jnp.where(here, turned(pack[i], 16 * i - 64), dense_e)
        dense[slot, 0] = dense_w
        dense[slot, 1] = dense_e
        for half in range(2):
            for j in range(GROUPS):
                rows = []
                for s in range(8):
                    l = half * 8 + s
                    if l < LEV:
                        rows.append(values[l, TILES - 1 + shift, 7:8, spans[j]])
                    elif l == LEV:
                        rows.append(msk[TILES - 1, 7:8, spans[j]].astype(F32))
                    else:
                        rows.append(jnp.zeros((1, LANES), F32))
                block = jnp.concatenate(rows, axis=0)
                top[slot, half * 8:half * 8 + 8, spans[GROUPS - 1 - j]] = lanes_of(block, flip)

    def exchange(base, to_west, to_east, to_fold, to_lo, to_hi, at):
        copies = [
            remote(to_fold, at[2], xs.at[base + 2], xr.at[base + 2], (comp, fold)),
            remote(to_west, at[0], xs.at[base], xr.at[base], (comp, west)),
            remote(to_east, at[1], xs.at[base + 1], xr.at[base + 1], (comp, east)),
        ]
        lo = remote(to_lo, at[3], xs.at[base + 3], xr.at[base + 3], (comp, fold_lo))
        hi = remote(to_hi, at[4], xs.at[base + 4], xr.at[base + 4], (comp, fold_hi))

        def start():
            for copy in copies:
                copy.start()

            @pl.when(fold_lo != tile)
            def _():
                lo.start()

            @pl.when(fold_hi != tile)
            def _():
                hi.start()

            @pl.when(fold_lo == tile)
            def _():
                at[3][...] = to_lo[...]

            @pl.when(fold_hi == tile)
            def _():
                at[4][...] = to_hi[...]

        def wait():
            for copy in copies:
                copy.wait_recv()

            @pl.when(fold_lo != tile)
            def _():
                lo.wait_recv()

            @pl.when(fold_hi != tile)
            def _():
                hi.wait_recv()

        def drain():
            for copy in copies:
                copy.wait_send()

            @pl.when(fold_lo != tile)
            def _():
                lo.wait_send()

            @pl.when(fold_hi != tile)
            def _():
                hi.wait_send()

        return start, wait, drain

    def halo_exchange(slot):
        return exchange(
            slot * 5, dense.at[slot, 0], dense.at[slot, 1], top.at[slot],
            dense.at[slot, 1], dense.at[slot, 0],
            [halo.at[slot, 0], halo.at[slot, 1], mirror.at[slot], halo.at[slot, 2], halo.at[slot, 3]],
        )

    def delta_exchange():
        return exchange(
            10, delta_out.at[0], delta_out.at[0], delta_out.at[1], delta_out.at[2], delta_out.at[2],
            [delta_in.at[n] for n in range(5)],
        )

    def fill_south():
        for l in range(LEV):
            st[l, 0, 7:8, :] = st[l, 1, 0:1, :]

    def fill_north(slot):
        for l in range(LEV):
            st[l, TILES + 1, 0:1, :] = mirror[slot, l:l + 1, :]

    def spread_sides(slot, summed):
        both = []
        for n in range(2):
            h = halo[slot, n]
            if summed:
                corner = pltpu.roll(halo[slot, 2 + n], 1, 0)
                following = jnp.where(lane >= LANES - 16, corner, turned(h, -16))
                previous = jnp.where(
                    lane < 16, jnp.broadcast_to(h[0:1], (SUB, LANES)), turned(h, 16)
                )
                h = row_pair_sum(h, following, previous)
            both.append(h)
        for i in range(TILES):
            sides_at[slot, i] = jnp.where(
                low_half, turned(both[0], -16 * i), turned(both[1], 64 - 16 * i)
            )

    def side_pick(halos, l):
        return lanes_of(halos, jnp.where(low_half, l, 64 + l))

    def row_sums(l, i):
        return [
            row_pair_sum(st[l, i + 1, :, span], st[l, i + 2, :, span], st[l, i, :, span])
            for span in spans
        ]

    def eliminate(i, l, j, value, carried):
        value = value * inv[l, i, :, spans[j]]
        if l > 0:
            value = value + elim[l - 1, i, :, spans[j]] * carried
        return value

    def back_substitute(i, j, partial):
        span = spans[j]
        result = partial[LEV - 1]
        u[LEV - 1, i, :, span] = result
        for l in range(LEV - 2, -1, -1):
            result = partial[l] + kap[l, i, :, span] * result
            u[l, i, :, span] = result

    def forward_first(i, carry):
        halos = sides_at[0, i]
        carried = [None] * GROUPS
        for l in range(LEV):
            sums = column_pair_sum(row_sums(l, i), side_pick(halos, l))
            for j in range(GROUPS):
                carried[j] = 0.25 * sums[j]
                if l < LEV - 1:
                    carried[j] = eliminate(i, l, j, carried[j], previous[j] if l else None)
                work[l, i, :, spans[j]] = carried[j]
            previous = list(carried)
        return carry

    def finish_first(i, groups):
        ys = [
            row_pair_sum(delta[i + 1, :, span], delta[i + 2, :, span], delta[i, :, span])
            for span in spans
        ]
        sums = column_pair_sum(ys, delta_side[i], groups)
        for j in groups:
            span = spans[j]
            partial = [work[l, i, :, span] for l in range(LEV - 1)]
            value = work[LEV - 1, i, :, span] + 0.25 * sums[j]
            partial.append(eliminate(i, LEV - 1, j, value, partial[-1]))
            back_substitute(i, j, partial)

    def finish_second(i, groups, ys_at, halos):
        carried = {j: None for j in groups}
        partial = {j: [] for j in groups}
        for l in range(LEV):
            sides = halos if halos is None else side_pick(halos, l)
            sums = column_pair_sum(ys_at(l), sides, groups)
            for j in groups:
                carried[j] = eliminate(i, l, j, 0.25 * sums[j], carried[j])
                partial[j].append(carried[j])
        for j in groups:
            back_substitute(i, j, partial[j])

    def second_middle(i, carry):
        def ys_at(l):
            ys = row_sums(l, i)
            for j in range(GROUPS):
                work[l, i, :, spans[j]] = ys[j]
            return ys

        finish_second(i, (1, 2), ys_at, None)
        return carry

    def second_sides(i, carry):
        def ys_at(l):
            return [work[l, i, :, span] for span in spans]

        finish_second(i, (0, 3), ys_at, sides_at[1, i])
        return carry

    def beside(x, left, right):
        from_east = jnp.where(lane_w == COLS - 1, right, pltpu.roll(x, COLS - 1, 1))
        from_west = jnp.where(lane_w == 0, left, pltpu.roll(x, 1, 1))
        return from_east, from_west

    def beyond(x, nxt, prev):
        upper = jnp.where(row_w == 7, jnp.broadcast_to(nxt, (SUB, COLS)), pltpu.roll(x, 7, 0))
        lower = jnp.where(row_w == 0, jnp.broadcast_to(prev, (SUB, COLS)), pltpu.roll(x, 1, 0))
        return upper, lower

    def ocean_sides(slot, i, l):
        right = jnp.broadcast_to(sides_at[slot, i, :, l:l + 1], (SUB, COLS))
        left = jnp.broadcast_to(sides_at[slot, i, :, 64 + l:65 + l], (SUB, COLS))
        return left, right

    def ocean_masks(i):
        wet = msk[i].astype(F32)
        m_e, m_w = beside(wet, *ocean_sides(0, i, LEV))
        nxt = jnp.where(
            i == TILES - 1, mirror[0, LEV:LEV + 1, :],
            msk[jnp.minimum(i + 1, TILES - 1), 0:1, :].astype(F32),
        )
        prev = jnp.where(i == 0, 0.0, msk[jnp.maximum(i - 1, 0), 7:8, :].astype(F32))
        m_n, m_s = beyond(wet, nxt, prev)
        return wet * m_e, wet * m_w, wet * m_n, wet * m_s

    def ocean_change(a, e, w, n, s, l, i, masks):
        d_e = masks[0] * (e - a)
        d_w = masks[1] * (w - a)
        d_n = masks[2] * (n - a)
        d_s = masks[3] * (s - a)
        return 0.15 * (d_e + d_w + d_n + d_s) - 0.25 * (
            vel[0, l, i] * (d_e - d_w) + vel[1, l, i] * (d_n - d_s)
        )

    def ocean_first(i, carry):
        masks = ocean_masks(i)
        for l in range(LEV):
            a = u[l, i]
            nxt = jnp.where(
                i == TILES - 1, mirror[0, l:l + 1, :], u[l, jnp.minimum(i + 1, TILES - 1), 0:1, :]
            )
            prev = jnp.where(i == 0, a[0:1], u[l, jnp.maximum(i - 1, 0), 7:8, :])
            e, w = beside(a, *ocean_sides(0, i, l))
            n, s = beyond(a, nxt, prev)
            change = ocean_change(a, e, w, n, s, l, i, masks)
            work[l, i] = change
            st[l, i + 1] = a + change
        return carry

    def ocean_second(i, carry):
        masks = ocean_masks(i)
        partial = [[] for _ in range(GROUPS)]
        carried = [None] * GROUPS
        for l in range(LEV):
            a = st[l, i + 1]
            e, w = beside(a, *ocean_sides(1, i, l))
            n, s = beyond(a, st[l, i + 2, 0:1, :], st[l, i, 7:8, :])
            change = ocean_change(a, e, w, n, s, l, i, masks)
            value = u[l, i] + 0.5 * (work[l, i] + change)
            if l == 0:
                value = value + delta[i + 1]
            for j in range(GROUPS):
                carried[j] = eliminate(i, l, j, value[:, spans[j]], carried[j])
                partial[j].append(carried[j])
        for j in range(GROUPS):
            back_substitute(i, j, partial[j])
        return carry

    for n in (2, 3, 5, 7, 8):
        loads[n].wait()
    high = deriv[...].astype(BF16)
    dmat[0:LANES, 0:LANES] = high
    dmat[0:LANES, LANES:2 * LANES] = (deriv[...] - high.astype(F32)).astype(BF16)
    dmat[LANES:2 * LANES, 0:LANES] = high
    dmat[LANES:2 * LANES, LANES:2 * LANES] = jnp.zeros((LANES, LANES), BF16)

    start_0, wait_0, drain_0 = halo_exchange(0)
    start_1, wait_1, drain_1 = halo_exchange(1)
    start_d, wait_d, drain_d = delta_exchange()

    @pl.when(is_ocean)
    def _():
        pack_edges(u, 0, 0, 1)
        start_0()

    def first_tendency(p, carry):
        tendency([(4 * p + r, j) for r in range(4) for j in range(GROUPS)], False)
        return carry

    @pl.when(is_atmos)
    def _():
        lax.fori_loop(0, TILES // 4, first_tendency, 0)
        pack_edges(st, 1, 0, 0)
        start_0()

    center.wait_recv()
    for copy in forwards:
        copy.start()

    loads[4].wait()
    loads[6].wait()
    lax.fori_loop(0, TILES, factors, 0, unroll=2)

    ident = ids[...]
    relative = (lax.shift_right_logical(ident, 8) - tile + 1 + N_TILE) & (N_TILE - 1)
    block = ident & (BLOCKS - 1)
    pos_v[...] = (
        jnp.minimum(relative, 2) * BLOCKS + (block & 3) * 64 + lax.shift_right_logical(block, 2)
    )
    pos_copy = local(pos_v, pos, lsem.at[9])
    pos_copy.start()

    pos_copy.wait()

    def widen(slot):
        for f in range(2):
            win[f, slot * BLOCKS:(slot + 1) * BLOCKS, :] = (
                winb[slot, f].reshape(BLOCKS, LANES).astype(F32)
            )

    widen(1)

    @pl.when(is_atmos)
    def _():
        wait_0()
        spread_sides(0, True)
        fill_south()
        fill_north(0)
        lax.fori_loop(0, TILES, forward_first, 0, unroll=4)

    @pl.when(is_ocean)
    def _():
        wait_0()
        spread_sides(0, False)
        lax.fori_loop(0, TILES, ocean_first, 0)
        pack_edges(st, 1, 1, 0)
        start_1()

    for copy in forwards:
        copy.wait_recv()
    widen(0)
    widen(2)

    def regrid_rows(j, b, rows_in):
        for s in rows_in:
            block = (b * 8 + s) * GROUPS + j
            sides = []
            for k in range(2):
                p = pos[k, block]
                rows = [win[0, pl.ds(p, 1), :], win[1, pl.ds(p, 1), :]]
                sides.append(jnp.concatenate(rows + rows[:1] * 6, axis=0))
            picked = jnp.concatenate(sides, axis=1).astype(BF16)
            tiles = jnp.concatenate([wbuf[j, b, s, 0], wbuf[j, b, s, 1]], axis=1)
            result = lax.dot_general(
                picked, tiles, (((1,), (1,)), ((), ())), preferred_element_type=F32
            )
            cpl[0, b, s:s + 1, spans[j]] = result[0:1]
            cpl[1, b, s:s + 1, spans[j]] = result[1:2]

    def regrid(j):
        def body(b, carry):
            regrid_rows(j, b, range(8))
            return carry

        lax.fori_loop(0, TILES, body, 0, unroll=8)

    for j in order:
        wloads[j].wait()

    def edge_delta(i, j, rows, pick):
        sums = [[], []]
        for s in range(SUB):
            block = (i * SUB + s) * GROUPS + j
            lines = [wbuf[j, i, s, k, rows, :].astype(F32)[pick:pick + 1] for k in range(2)]
            for f in range(2):
                sums[f].append(
                    lines[0] * win[f, pl.ds(pos[0, block], 1), :]
                    + lines[1] * win[f, pl.ds(pos[1, block], 1), :]
                )
        target, wind = [
            jnp.broadcast_to(
                jnp.sum(jnp.concatenate(part, axis=0), axis=1, keepdims=True), (SUB, LANES)
            )
            for part in sums
        ]
        return rate_of(i, spans[j], wind) * (target - surf[0, i, :, spans[j]])

    def edge_pack(i, packed):
        left = edge_delta(i, 0, slice(0, 16), 0)
        right = edge_delta(i, GROUPS - 1, slice(LANES - 16, LANES), 15)
        return jnp.where((lane & 63) == i, side_pack(left, right), packed)

    for j in range(GROUPS):
        regrid_rows(j, TILES - 1, (SUB - 1,))
    rows = [delta_at(TILES - 1, spans[j])[7:8] for j in range(GROUPS - 1, -1, -1)]
    delta_out[1] = lanes_of(jnp.concatenate(rows + rows, axis=0), flip)
    packed = lax.fori_loop(0, TILES, edge_pack, jnp.zeros((SUB, LANES), F32), unroll=4)
    delta_out[0] = packed
    delta_out[2, 0:1, :] = pltpu.roll(packed, 64, 1)[SUB - 1:SUB]
    start_d()
    for j in order:
        regrid(j)

    def all_delta(i, carry):
        for span in spans:
            delta[i + 1, :, span] = delta_at(i, span)
        return carry

    lax.fori_loop(0, TILES, all_delta, 0)

    wait_d()
    sides = jnp.where(low_half, delta_in[0], delta_in[1])
    for j in range(GROUPS):
        delta[TILES + 1, 0:1, spans[j]] = delta_in[2, j:j + 1, :]
    delta[0, 7:8, :] = delta[1, 0:1, :]

    @pl.when(is_atmos)
    def _():
        corner = jnp.where(low_half, delta_in[3], delta_in[4])
        following = jnp.where((lane & 63) == TILES - 1, corner, pltpu.roll(sides, LANES - 1, 1))
        previous = jnp.where(
            (lane & 63) == 0, jnp.broadcast_to(sides[0:1], (SUB, LANES)), pltpu.roll(sides, 1, 1)
        )
        summed = row_pair_sum(sides, following, previous)
        for i in range(TILES):
            delta_side[i] = side_pick(summed, i)

        last = TILES - 1

        def finish_sides(i, carry):
            finish_first(i, (0, 3))
            return carry

        def finish_inner(i, carry):
            finish_first(i, (1, 2))
            return carry

        def tend_sides(p, carry):
            tendency([(4 * p + r, j) for r in range(4) for j in (0, 3)], True)
            return carry

        def tend_inner(p, carry):
            tendency([(4 * p + r, j) for r in range(4) for j in (1, 2)], True)
            return carry

        lax.fori_loop(0, TILES, finish_sides, 0, unroll=4)
        finish_first(last, (1, 2))
        tendency([(last, 1), (last, 2)], True)
        lax.fori_loop(0, TILES // 4, tend_sides, 0)
        pack_edges(st, 1, 1, 0)
        start_1()
        lax.fori_loop(0, last, finish_inner, 0, unroll=7)
        lax.fori_loop(0, TILES // 4, tend_inner, 0)
        fill_south()
        lax.fori_loop(0, last, second_middle, 0, unroll=7)
        wait_1()
        spread_sides(1, True)
        fill_north(1)
        for l in range(LEV):
            ys = row_sums(l, last)
            for j in range(GROUPS):
                work[l, last, :, spans[j]] = ys[j]
        lax.fori_loop(0, TILES, second_sides, 0, unroll=4)
        finish_second(last, (1, 2), lambda l: [work[l, last, :, span] for span in spans], None)

    @pl.when(is_ocean)
    def _():
        wait_1()

        def add_forcing(i, carry):
            st[0, i + 1] = st[0, i + 1] + delta[i + 1]
            return carry

        lax.fori_loop(0, TILES, add_forcing, 0)
        mirror[1, 0:1, :] = mirror[1, 0:1, :] + delta[TILES + 1, 0:1, :]
        fill_south()
        fill_north(1)
        spread_sides(1, False)
        for i in range(TILES):
            sides_at[1, i] = sides_at[1, i] + jnp.where(
                (lane & 63) == 0, side_pick(sides, i), 0.0
            )
        lax.fori_loop(0, TILES, ocean_second, 0)

    center.wait_send()
    for copy in forwards:
        copy.wait_send()
    drain_0()
    drain_d()
    drain_1()


def on_device(fields, velocity, mixing, surface_mask, intersection_ids, intersection_weights):
    vmem = pl.BlockSpec(memory_space=pltpu.VMEM)
    hbm = pl.BlockSpec(memory_space=pltpu.HBM)
    scratch = [
        pltpu.VMEM((2, LEV, TILES, SUB, COLS), F32),
        pltpu.VMEM((LEV - 1, TILES, SUB, COLS), F32),
        pltpu.VMEM((LEV - 1, TILES, SUB, COLS), F32),
        pltpu.VMEM((TILES, SUB, COLS), jnp.int32),
        pltpu.VMEM((GROUPS, TILES, SUB, 2, LANES, LANES), BF16),
        pltpu.VMEM((2, TILES, SUB, COLS), F32),
        pltpu.VMEM((2, GROUPS, 64, LANES), BF16),
        pltpu.VMEM((3, 2, GROUPS, 64, LANES), BF16),
        pltpu.VMEM((2, 3 * BLOCKS, LANES), F32),
        pltpu.VMEM((LEV, TILES + 2, SUB, COLS), F32),
        pltpu.VMEM((LEV, TILES, SUB, COLS), F32),
        pltpu.VMEM((LEV, TILES, SUB, COLS), F32),
        pltpu.VMEM((2, BLOCKS), jnp.int32),
        pltpu.VMEM((2, BLOCKS), jnp.int32),
        pltpu.SMEM((2, BLOCKS), jnp.int32),
        pltpu.VMEM((4, SUB, LANES), F32),
        pltpu.VMEM((LANES, LANES), F32),
        pltpu.VMEM((2 * LANES, 2 * LANES), BF16),
        pltpu.VMEM((TILES, SUB, LANES), F32),
        pltpu.VMEM((2, 2, SUB, LANES), F32),
        pltpu.VMEM((2, 16, COLS), F32),
        pltpu.VMEM((2, 4, SUB, LANES), F32),
        pltpu.VMEM((2, TILES, SUB, LANES), F32),
        pltpu.VMEM((2, 16, COLS), F32),
        pltpu.VMEM((TILES + 2, SUB, COLS), F32),
        pltpu.VMEM((3, SUB, LANES), F32),
        pltpu.VMEM((5, SUB, LANES), F32),
        pltpu.VMEM((TILES, SUB, LANES), F32),
        pltpu.SemaphoreType.DMA((10,)),
        pltpu.SemaphoreType.DMA((GROUPS,)),
        pltpu.SemaphoreType.DMA((3,)),
        pltpu.SemaphoreType.DMA((3,)),
        pltpu.SemaphoreType.DMA((15,)),
        pltpu.SemaphoreType.DMA((15,)),
    ]
    advanced, coupled = pl.pallas_call(
        kernel,
        out_shape=(
            pltpu.VMEM((LEV, TILES, SUB, COLS), F32),
            pltpu.VMEM((2, TILES, SUB, COLS), F32),
        ),
        in_specs=[hbm] * 8,
        out_specs=(vmem, vmem),
        scratch_shapes=scratch,
        compiler_params=pltpu.CompilerParams(
            collective_id=0, has_side_effects=True, vmem_limit_bytes=52 << 20
        ),
    )(
        jnp.transpose(intersection_ids[0], (1, 0)),
        jnp.asarray(across_table()),
        jnp.asarray(along_matrix()),
        fields.reshape(LEV, TILES, SUB, COLS),
        velocity.reshape(2, LEV, TILES, SUB, COLS),
        mixing.reshape(LEV - 1, TILES, SUB, COLS),
        surface_mask.reshape(TILES, SUB, COLS),
        intersection_weights.reshape(TILES, SUB, GROUPS, 2, LANES, LANES),
    )
    return (
        advanced.reshape(1, LEV, TILES * SUB, COLS),
        coupled.reshape(1, 2, TILES * SUB, COLS),
    )


def solution(mesh):
    placed = (
        P("comp", None, None, "tile"),
        P("comp", None, None, None, "tile"),
        P("comp", None, None, "tile"),
        P("comp", None, "tile"),
        P("comp", "tile", None),
        P("comp", "tile", None, None, None),
    )
    return jax.shard_map(
        on_device,
        mesh=mesh,
        in_specs=placed,
        out_specs=(P("comp", None, None, "tile"), P("comp", None, None, "tile")),
        check_vma=False,
    )
```
